512 devices in a mesh: row: 64 (over y, z), col: 8 (over x, core).
Axes of the slice: x: 4, y: 8, z: 8, core: 2. Of those that a mesh axis runs over, the one named last changes fastest.
Arguments:
- features: bfloat16 [65536, 512], P(('row', 'col')), may hold values from -6 to 6
- weight: bfloat16 [512, 512], replicated, may hold values from -0.25 to 0.25
- bias_vec: float32 [512], replicated, may hold values from -3 to 3
- tile_vals: bfloat16 [64, 8, 16, 128, 128], P('row', 'col'), may hold values from -0.1875 to 0.1875
- tile_coords: int32 [64, 8, 16, 2], P('row', 'col'), may hold values from 0 to 63, as said below
- tile_count: int32 [64, 8], P('row', 'col'), may hold values from 2 to 16, as said below
- cotangent: bfloat16 [65536, 512], P(('row', 'col')), may hold values from -6 to 6
Outputs:
- layer_out: bfloat16 [65536, 512], P(('row', 'col'))
- grad_weight: float32 [512, 512], replicated
- grad_bias: float32 [512], replicated
- grad_features: bfloat16 [65536, 512], P(('row', 'col'))
The draws below stay inside these ranges and needn't reach their ends.
Inputs may be any that keep to these rules, and one draw needn't show every extreme that they name: tile_coords[r, c, s, 0] is below 8; tile_coords[r, c, s, 1] lies in the row bands r - 3 to r + 3 that exist. `tile_count`: some device has all 16 slots live.
All inputs are finite; a program needn't handle non-finite values.
Results may differ from the reference program's by a relative error of at most 0.019.
Values may be sent and summed in bfloat16 or wider, within the bound.
No kernel may reach another device: no remote copies, remote signals or barrier semaphores. Data moves between devices by JAX's collectives and lax.ppermute only.
A program may use at most 64 MiB of HBM per device.

```python
import jax
import jax.numpy as jnp
from jax import lax

F = 512
TILE = 128
TILE_SLOTS = 16
REACH = 3
NODES = 65536
N_ROW = 64
N_COL = 8


def draw_tile_coords(key, part):
    key_rows, key_cols = jax.random.split(jax.random.fold_in(key, 11))
    rows_local = jax.random.randint(key_rows, (N_ROW, N_COL, TILE_SLOTS), 0, N_COL)
    offsets = jax.random.randint(key_cols, (N_ROW, N_COL, TILE_SLOTS), -REACH, REACH + 1)
    band_idx = jnp.arange(N_ROW, dtype=jnp.int32)[:, None, None]
    cols_local = jnp.clip(band_idx + offsets, 0, N_ROW - 1)
    return jnp.stack([rows_local, cols_local], axis=-1).astype(jnp.int32)


def draw_tile_count(key, part):
    key_base, key_full, key_pick = jax.random.split(jax.random.fold_in(key, 23), 3)
    base_count = jax.random.randint(key_base, (N_ROW, N_COL), TILE_SLOTS // 8, TILE_SLOTS // 2 + 1)
    full_mask = jax.random.randint(key_full, (N_ROW, N_COL), 0, 8) == 0
    picked = jax.random.randint(key_pick, (), 0, N_ROW * N_COL)
    forced = jnp.arange(N_ROW * N_COL, dtype=jnp.int32).reshape(N_ROW, N_COL) == picked
    return jnp.where(full_mask | forced, TILE_SLOTS, base_count).astype(jnp.int32)


def levels(own_key, extent, cuts, low, high):
    level = 1.0
    for dim, parts in cuts:
        heights = jax.random.uniform(jax.random.fold_in(jax.random.fold_in(own_key, 6), dim), (parts,), jnp.float32, low / len(cuts), high / len(cuts))
        level = level * jnp.repeat(jnp.exp(heights), extent[dim] // parts).reshape((-1,) + (1,) * (len(extent) - 1 - dim))
    return level


def bell_draw(rng, dims, spread, limit, cuts=(), kind=jnp.bfloat16):
    array = spread * jax.random.normal(rng, dims, jnp.float32)
    if cuts:
        array = array * levels(rng, dims, cuts, -0.22, 0.18)
    return jnp.clip(array, -limit, limit).astype(kind)


def setup_inputs(seed: int = 0) -> dict:
    streams_of = jax.random.split(jax.random.key(seed), 8)
    return {
        "features": bell_draw(streams_of[0], (NODES, F), 1.0, 6.0, ((0, 512),)),
        "weight": bell_draw(streams_of[1], (F, F), F ** -0.5, 0.25),
        "bias_vec": bell_draw(streams_of[2], (F,), 0.5, 3.0, (), jnp.float32),
        "tile_vals": bell_draw(streams_of[3], (N_ROW, N_COL, TILE_SLOTS, TILE, TILE), (TILE * TILE_SLOTS // 2) ** -0.5, 0.1875, ((0, 64), (1, 8))),
        "tile_coords": draw_tile_coords(jax.random.fold_in(streams_of[7], 71), 0),
        "tile_count": draw_tile_count(jax.random.fold_in(streams_of[7], 71), 0),
        "cotangent": bell_draw(streams_of[6], (NODES, F), 1.0, 6.0, ((0, 512),)),
    }


def gelu_tanh(values):
    return jax.nn.gelu(values, approximate=True)

def place_tiles(tile_coords, tile_count):
    band_idx = jnp.arange(N_ROW, dtype=jnp.int32)[:, None, None]
    group_idx = jnp.arange(N_COL, dtype=jnp.int32)[None, :, None]
    row_glob = (band_idx * N_COL + tile_coords[..., 0]).astype(jnp.int32).reshape(N_ROW * N_COL, TILE_SLOTS)
    col_glob = (tile_coords[..., 1] * N_COL + group_idx).astype(jnp.int32).reshape(N_ROW * N_COL, TILE_SLOTS)
    slot_idx = jnp.arange(TILE_SLOTS, dtype=jnp.int32)[None, None, :]
    alive_mask = (slot_idx < tile_count[:, :, None]).astype(jnp.float32).reshape(N_ROW * N_COL, TILE_SLOTS)
    return (row_glob, col_glob, alive_mask)

def reference(features, weight, bias_vec, tile_vals, tile_coords, tile_count, cotangent):
    block_total = N_ROW * N_COL
    row_glob, col_glob, alive_mask = place_tiles(tile_coords, tile_count)
    tile_flat = tile_vals.reshape(block_total, TILE_SLOTS, TILE, TILE)
    panels = features.reshape(block_total, TILE, F).astype(jnp.float32)

    def forward_step(totals, operands):
        tiles_now, rows_now, cols_now, alive_now = operands
        product = jnp.einsum('sij,sjf->sif', tiles_now.astype(jnp.float32), panels[cols_now])
        return (totals.at[rows_now].add(product * alive_now[:, None, None]), None)
    aggregate, unused = lax.scan(forward_step, jnp.zeros((block_total, TILE, F), jnp.float32), (tile_flat, row_glob, col_glob, alive_mask))
    aggregate_b = aggregate.reshape(NODES, F).astype(jnp.bfloat16)
    pre_act = jnp.dot(aggregate_b, weight, preferred_element_type=jnp.float32) + bias_vec
    layer_out = gelu_tanh(pre_act).astype(jnp.bfloat16)
    unused_out, pullback = jax.vjp(gelu_tanh, pre_act)
    grad_pre = pullback(cotangent.astype(jnp.float32))[0].astype(jnp.bfloat16)
    grad_weight = jnp.einsum('nf,ng->fg', aggregate_b.astype(jnp.float32), grad_pre.astype(jnp.float32))
    grad_bias = lax.optimization_barrier(jnp.sum(grad_pre.astype(jnp.float32), axis=0))
    grad_mid = jnp.einsum('ng,fg->nf', grad_pre.astype(jnp.float32), weight.astype(jnp.float32)).astype(jnp.bfloat16)
    mid_panels = grad_mid.reshape(block_total, TILE, F).astype(jnp.float32)

    def backward_step(totals, operands):
        tiles_now, rows_now, cols_now, alive_now = operands
        product = jnp.einsum('sji,sjf->sif', tiles_now.astype(jnp.float32), mid_panels[rows_now])
        return (totals.at[cols_now].add(product * alive_now[:, None, None]), None)
    grad_acc, unused_two = lax.scan(backward_step, jnp.zeros((block_total, TILE, F), jnp.float32), (tile_flat, row_glob, col_glob, alive_mask))
    grad_features = grad_acc.reshape(NODES, F).astype(jnp.bfloat16)
    return (layer_out, grad_weight, grad_bias, grad_features)
```

```python
import jax
import jax.numpy as jnp
from jax import lax
from jax.experimental import pallas as pl
from jax.experimental.pallas import tpu as pltpu
from jax.sharding import Mesh, PartitionSpec as P

REACH = 3
WINDOW = 2 * REACH + 1
TILE = 128
FEAT = 512
BANDS = 8
SLOTS = 16
ROW = ("y", "z")
COL = ("x", "core")
ALL = ("y", "z", "x", "core")
EXTRA = 128
BF16 = jnp.bfloat16
F32 = jnp.float32
SQRT_2_OVER_PI = 0.7978845608028654
VMEM_LIMIT = 48 * 1024 * 1024

SMEM_SPEC = pl.BlockSpec(memory_space=pltpu.SMEM)
VMEM_SPEC = pl.BlockSpec(memory_space=pltpu.VMEM)
ANY_SPEC = pl.BlockSpec(memory_space=pl.ANY)


def params():
    return pltpu.CompilerParams(vmem_limit_bytes=VMEM_LIMIT)


def rolled(block, axis, distance):
    size = lax.axis_size(axis)
    return lax.ppermute(block, axis, [(i, (i + distance) % size) for i in range(size)])


def exchange(chunks, axis):
    return lax.all_to_all(chunks, axis, 0, 0, tiled=True)


def copy_in(sources, targets, sems):
    copies = [
        pltpu.make_async_copy(s, t, sems.at[i]) for i, (s, t) in enumerate(zip(sources, targets))
    ]
    for c in copies:
        c.start()
    return copies


def forward_kernel(meta, tiles_hbm, *refs):
    panel_refs = refs[:WINDOW]
    out, tiles, panels, acc, sems = refs[WINDOW:]
    copies = copy_in(
        [tiles_hbm, *panel_refs], [tiles, *[panels.at[i] for i in range(WINDOW)]], sems
    )
    acc[...] = jnp.zeros_like(acc)
    for c in copies:
        c.wait()

    def slot(s, carry):
        b = meta[s]
        w = meta[SLOTS + s]
        acc[b] += jnp.dot(tiles[s], panels[w], preferred_element_type=F32)
        return carry

    lax.fori_loop(0, meta[2 * SLOTS], slot, 0)
    out[...] = acc[...].astype(BF16)


def forward(meta, tiles, panels):
    return pl.pallas_call(
        forward_kernel,
        out_shape=jax.ShapeDtypeStruct((BANDS, TILE, FEAT), BF16),
        in_specs=[SMEM_SPEC] + [ANY_SPEC] * (1 + WINDOW),
        out_specs=VMEM_SPEC,
        scratch_shapes=[
            pltpu.VMEM((SLOTS, TILE, TILE), BF16),
            pltpu.VMEM((WINDOW, TILE, FEAT), BF16),
            pltpu.VMEM((BANDS, TILE, FEAT), F32),
            pltpu.SemaphoreType.DMA((1 + WINDOW,)),
        ],
        compiler_params=params(),
        name="aggregate_tiles",
    )(meta, tiles, *panels)


def bias_rows(total):
    high = total.astype(BF16).astype(F32)
    return jnp.concatenate([high, total - high, jnp.zeros((8, 128), F32)], axis=0).astype(BF16)


def dense_kernel(parts, weight, bias, cot, layer_out, grad_mid, chunks):
    agg = parts[0].astype(F32)
    for i in range(1, BANDS):
        agg = agg + parts[i].astype(F32)
    agg_b = agg.astype(BF16)
    w = weight[...]
    v = jnp.dot(agg_b, w, preferred_element_type=F32) + bias[...]
    v2 = v * v
    t = jnp.tanh(SQRT_2_OVER_PI * (v + 0.044715 * (v2 * v)))
    half = 0.5 * (1.0 + t)
    layer_out[...] = (v * half).astype(BF16)
    slope = half + 0.5 * v * (1.0 - t * t) * (SQRT_2_OVER_PI * (1.0 + 3 * 0.044715 * v2))
    grad_pre = (cot[...].astype(F32) * slope).astype(BF16)
    grad_mid[...] = lax.dot_general(
        grad_pre, w, (((1,), (1,)), ((), ())), preferred_element_type=F32
    ).astype(BF16)
    term = lax.dot_general(agg_b, grad_pre, (((0,), (0,)), ((), ())), preferred_element_type=F32)
    count = chunks.shape[0]
    chunks[:, :, :FEAT] = term.astype(BF16).reshape(count, FEAT // count, FEAT)
    total = jnp.sum(grad_pre.astype(F32), axis=0, keepdims=True)
    total = jnp.concatenate([total[:, i * 128 : (i + 1) * 128] for i in range(4)], axis=0)
    chunks[:, :, FEAT:] = jnp.broadcast_to(bias_rows(total)[None], (count, 16, EXTRA))


def dense(parts, weight, bias, cot, groups):
    return pl.pallas_call(
        dense_kernel,
        out_shape=(
            jax.ShapeDtypeStruct((TILE, FEAT), BF16),
            jax.ShapeDtypeStruct((TILE, FEAT), BF16),
            jax.ShapeDtypeStruct((groups, FEAT // groups, FEAT + EXTRA), BF16),
        ),
        in_specs=[VMEM_SPEC] * 4,
        out_specs=(VMEM_SPEC,) * 3,
        compiler_params=params(),
        name="dense_layer",
    )(parts, weight, bias, cot)


def backward_kernel(meta, tiles_hbm, same_hbm, other_hbm, *refs):
    outs = refs[:WINDOW]
    tiles, panels, acc, sems = refs[WINDOW:]
    copies = copy_in(
        [tiles_hbm, same_hbm, other_hbm], [tiles, panels.at[0], panels.at[1]], sems
    )
    acc[...] = jnp.zeros_like(acc)
    for c in copies:
        c.wait()

    def slot(s, carry):
        b = meta[s]
        w = meta[SLOTS + s]
        side = (b + meta[2 * SLOTS + 1]) & 1
        acc[w] += lax.dot_general(
            tiles[s], panels[side, b >> 1], (((0,), (0,)), ((), ())), preferred_element_type=F32
        )
        return carry

    lax.fori_loop(0, meta[2 * SLOTS], slot, 0)
    for i in range(WINDOW):
        outs[i][...] = acc[i].astype(outs[i].dtype)


def backward(meta, tiles, same, other):
    return pl.pallas_call(
        backward_kernel,
        out_shape=tuple(
            jax.ShapeDtypeStruct((TILE, FEAT), F32 if i == REACH else BF16) for i in range(WINDOW)
        ),
        in_specs=[SMEM_SPEC] + [ANY_SPEC] * 3,
        out_specs=(VMEM_SPEC,) * WINDOW,
        scratch_shapes=[
            pltpu.VMEM((SLOTS, TILE, TILE), BF16),
            pltpu.VMEM((2, BANDS // 2, TILE, FEAT), BF16),
            pltpu.VMEM((WINDOW, TILE, FEAT), F32),
            pltpu.SemaphoreType.DMA((3,)),
        ],
        compiler_params=params(),
        name="backward_tiles",
    )(meta, tiles, same, other)


def summed(parts):
    total = parts[0].astype(F32)
    for i in range(1, parts.shape[0]):
        total = total + parts[i].astype(F32)
    return total


def middle_kernel(parts, out):
    total = summed(parts)
    out[:, :, :FEAT] = jnp.broadcast_to(total[None, :, :FEAT].astype(BF16), (out.shape[0], 16, FEAT))
    bias = total[0:4, FEAT:] + total[4:8, FEAT:]
    out[:, :, FEAT:] = jnp.broadcast_to(bias_rows(bias)[None], (out.shape[0], 16, EXTRA))


def middle_sum(parts, copies):
    return pl.pallas_call(
        middle_kernel,
        out_shape=jax.ShapeDtypeStruct((copies, 16, FEAT + EXTRA), BF16),
        in_specs=[VMEM_SPEC],
        out_specs=VMEM_SPEC,
        compiler_params=params(),
        name="group_sum",
    )(parts)


def last_kernel(parts, out, bias_out):
    total = summed(parts)
    out[...] = jnp.broadcast_to(total[None, :, :FEAT].astype(BF16), out.shape)
    bias = total[0:4, FEAT:] + total[4:8, FEAT:]
    for i in range(4):
        bias_out[:, i * 128 : (i + 1) * 128] = bias[i : i + 1]


def last_sum(parts, copies):
    return pl.pallas_call(
        last_kernel,
        out_shape=(
            jax.ShapeDtypeStruct((copies, 16, FEAT), BF16),
            jax.ShapeDtypeStruct((1, FEAT), F32),
        ),
        in_specs=[VMEM_SPEC],
        out_specs=(VMEM_SPEC,) * 2,
        compiler_params=params(),
        name="total_sum",
    )(parts)


def body(features, weight, bias_vec, tile_vals, tile_coords, tile_count, cotangent):
    own_row = lax.axis_index(ROW)
    core = lax.axis_index("core")
    tiles = tile_vals[0, 0]
    coords = tile_coords[0, 0]
    meta = jnp.concatenate(
        [
            coords[:, 0],
            coords[:, 1] - own_row + REACH,
            tile_count.reshape(1),
            core.reshape(1).astype(jnp.int32),
        ]
    )
    near = {0: features}
    for d in (1, 2, 3, -1, -2, -3):
        near[-d] = rolled(features, ROW, d)
    partial = forward(meta, tiles, [near[i - REACH] for i in range(WINDOW)])
    parts = exchange(partial, COL)
    groups = lax.axis_size("z") * lax.axis_size("x")
    copies = lax.axis_size("y") * lax.axis_size("core")
    layer_out, grad_mid, chunks = dense(parts, weight, bias_vec.reshape(1, FEAT), cotangent, groups)

    same = lax.all_gather(grad_mid, "x", axis=0, tiled=False)
    other = rolled(same, "core", 1)
    grads = backward(meta, tiles, same, other)
    result = grads[REACH]
    for d in (1, 2, 3, -1, -2, -3):
        result = result + rolled(grads[REACH + d], ROW, d).astype(F32)
    grad_features = result.astype(BF16)

    spread = middle_sum(exchange(chunks, ("z", "x")), copies)
    final, bias_total = last_sum(exchange(spread, ("y", "core")), groups)
    grad_weight = exchange(final, ("z", "x")).reshape(FEAT, FEAT).astype(F32)
    return (layer_out, grad_weight, bias_total.reshape(FEAT), grad_features)


def solution(mesh):
    split = Mesh(mesh.devices.reshape(8, 8, 4, 2), ALL)
    return jax.shard_map(
        body,
        mesh=split,
        in_specs=(
            P(ALL, None),
            P(),
            P(),
            P(ROW, COL, None, None, None),
            P(ROW, COL, None, None),
            P(ROW, COL),
            P(ALL, None),
        ),
        out_specs=(P(ALL, None), P(), P(), P(ALL, None)),
        check_vma=False,
    )
```

```python
import jax
import jax.numpy as jnp
from jax import lax
from jax.experimental import pallas as pl
from jax.experimental.pallas import tpu as pltpu
from jax.sharding import Mesh, PartitionSpec as P

REACH = 3
WINDOW = 2 * REACH + 1
TILE = 128
FEAT = 512
BANDS = 8
SLOTS = 16
ROW = ("y", "z", "pair")
COL = ("x", "core")
ALL = ROW + COL
PAIR = "pair"
SPREAD = ("y", "x")
REST = ("z", "pair")
EXTRA = 128
HALF = 256
BF16 = jnp.bfloat16
F32 = jnp.float32
SQRT_2_OVER_PI = 0.7978845608028654
VMEM_LIMIT = 40 * 1024 * 1024

SMEM_SPEC = pl.BlockSpec(memory_space=pltpu.SMEM)
VMEM_SPEC = pl.BlockSpec(memory_space=pltpu.VMEM)
ANY_SPEC = pl.BlockSpec(memory_space=pl.ANY)
HBM_SPEC = pl.BlockSpec(memory_space=pltpu.HBM)


def params():
    return pltpu.CompilerParams(vmem_limit_bytes=VMEM_LIMIT)


def moved(block, target):
    size = lax.axis_size(ROW)
    return lax.ppermute(block, ROW, [(i, target(i) % size) for i in range(size)])


def to_sibling(i):
    return i ^ 1


def to_odd(i):
    return i + 1 if i % 2 else i - 1


def to_skip(i):
    return i + 2 if i % 2 else i - 2


def from_skip(i):
    return i - 2 if i % 2 else i + 2


def to_far(i):
    return i + 3 if i % 2 else i - 3


def swapped(block):
    return lax.ppermute(block, "core", [(0, 1), (1, 0)])


def exchange(chunks, axis):
    return lax.all_to_all(chunks, axis, 0, 0, tiled=True)


def copy_in(sources, targets, sems):
    copies = [
        pltpu.make_async_copy(s, t, sems.at[i]) for i, (s, t) in enumerate(zip(sources, targets))
    ]
    for c in copies:
        c.start()
    return copies


def stage_kernel(source, out, sem):
    copy = pltpu.make_async_copy(source, out, sem)
    copy.start()
    copy.wait()


def stage(tiles):
    return pl.pallas_call(
        stage_kernel,
        out_shape=jax.ShapeDtypeStruct(tiles.shape, tiles.dtype),
        in_specs=[HBM_SPEC],
        out_specs=VMEM_SPEC,
        scratch_shapes=[pltpu.SemaphoreType.DMA],
        compiler_params=params(),
        name="stage_tiles",
    )(tiles)


def forward_kernel(meta, tiles, own, odd, skip, far, mine, theirs, panels, acc, sems):
    copies = copy_in(
        [own, odd, skip, far],
        [panels.at[0:2], panels.at[2:4], panels.at[4:6], panels.at[6:7]],
        sems,
    )
    acc[...] = jnp.zeros_like(acc)
    for c in copies:
        c.wait()

    def slot(s, carry):
        acc[meta[s]] += jnp.dot(tiles[s], panels[meta[SLOTS + s]], preferred_element_type=F32)
        return carry

    lax.fori_loop(0, meta[2 * SLOTS], slot, 0)
    mine[...] = acc[0:4]
    theirs[...] = acc[4:8].astype(BF16)


def forward(meta, tiles, own, odd, skip, far):
    return pl.pallas_call(
        forward_kernel,
        out_shape=(
            jax.ShapeDtypeStruct((BANDS // 2, TILE, FEAT), F32),
            jax.ShapeDtypeStruct((BANDS // 2, TILE, FEAT), BF16),
        ),
        in_specs=[SMEM_SPEC, VMEM_SPEC] + [ANY_SPEC] * 4,
        out_specs=(VMEM_SPEC,) * 2,
        scratch_shapes=[
            pltpu.VMEM((WINDOW, TILE, FEAT), BF16),
            pltpu.VMEM((BANDS, TILE, FEAT), F32),
            pltpu.SemaphoreType.DMA((4,)),
        ],
        compiler_params=params(),
        name="aggregate_tiles",
    )(meta, tiles, own, odd, skip, far)


def bias_rows(total):
    high = total.astype(BF16).astype(F32)
    return jnp.concatenate([high, total - high, jnp.zeros((8, 128), F32)], axis=0).astype(BF16)


def dense_kernel(core, parts, weight, bias, cot, layer_out, mids, mine, theirs, terms):
    agg = parts[0].astype(F32)
    for i in range(1, BANDS // 2):
        agg = agg + parts[i].astype(F32)
    agg_b = agg.astype(BF16)
    w = weight[...]
    v = jnp.dot(agg_b, w, preferred_element_type=F32) + bias[...]
    v2 = v * v
    t = jnp.tanh(SQRT_2_OVER_PI * (v + 0.044715 * (v2 * v)))
    half = 0.5 * (1.0 + t)
    layer_out[...] = (v * half).astype(BF16)
    slope = half + 0.5 * v * (1.0 - t * t) * (SQRT_2_OVER_PI * (1.0 + 3 * 0.044715 * v2))
    grad_pre = (cot[...].astype(F32) * slope).astype(BF16)
    mid = lax.dot_general(
        grad_pre, w, (((1,), (1,)), ((), ())), preferred_element_type=F32
    ).astype(BF16)
    mids[...] = jnp.broadcast_to(mid[None], mids.shape)
    term = lax.dot_general(agg_b, grad_pre, (((0,), (0,)), ((), ())), preferred_element_type=F32)
    count = mine.shape[0] - 1
    for i in range(2):
        terms[i] = term[:, i * HALF : (i + 1) * HALF].reshape(count, 16, HALF)
    k = core[0]
    mine[0:count] = terms[k]
    theirs[0:count] = terms[1 - k].astype(BF16)
    total = jnp.sum(grad_pre.astype(F32), axis=0, keepdims=True)
    total = jnp.concatenate([total[:, i * 128 : (i + 1) * 128] for i in range(4)], axis=0)
    zeros = jnp.zeros((16, HALF - EXTRA), F32)
    mine[count] = jnp.concatenate([bias_rows(total).astype(F32), zeros], axis=1)
    theirs[count] = jnp.concatenate([bias_rows(total), zeros.astype(BF16)], axis=1)


def dense(core, parts, weight, bias, cot, groups):
    return pl.pallas_call(
        dense_kernel,
        out_shape=(
            jax.ShapeDtypeStruct((TILE, FEAT), BF16),
            jax.ShapeDtypeStruct((BANDS // 2, TILE, FEAT), BF16),
            jax.ShapeDtypeStruct((groups + 1, 16, HALF), F32),
            jax.ShapeDtypeStruct((groups + 1, 16, HALF), BF16),
        ),
        in_specs=[SMEM_SPEC] + [VMEM_SPEC] * 4,
        out_specs=(VMEM_SPEC,) * 4,
        scratch_shapes=[pltpu.VMEM((2, groups, 16, HALF), F32)],
        compiler_params=params(),
        name="dense_layer",
    )(core, parts, weight, bias, cot)


def chip_kernel(mine, theirs, out):
    count = out.shape[0]
    out[:, :, :HALF] = (mine[0:count] + theirs[0:count].astype(F32)).astype(BF16)
    both = mine[count, :, :EXTRA] + theirs[count, :, :EXTRA].astype(F32)
    bias = bias_rows(both[0:4] + both[4:8])
    out[:, :, HALF:] = jnp.broadcast_to(bias[None], (count, 16, EXTRA))


def chip_sum(mine, theirs):
    count = mine.shape[0] - 1
    return pl.pallas_call(
        chip_kernel,
        out_shape=jax.ShapeDtypeStruct((count, 16, HALF + EXTRA), BF16),
        in_specs=[VMEM_SPEC] * 2,
        out_specs=VMEM_SPEC,
        compiler_params=params(),
        name="chip_sum",
    )(mine, theirs)


def backward_kernel(meta, tiles, same, other, own, odd, skip, far, panels, acc, sems):
    copies = copy_in([same, other], [panels.at[0:4], panels.at[4:8]], sems)
    acc[...] = jnp.zeros_like(acc)
    for c in copies:
        c.wait()

    def slot(s, carry):
        acc[meta[SLOTS + s]] += lax.dot_general(
            tiles[s], panels[meta[s]], (((0,), (0,)), ((), ())), preferred_element_type=F32
        )
        return carry

    lax.fori_loop(0, meta[2 * SLOTS], slot, 0)
    own[...] = acc[0:2]
    odd[...] = acc[2:4].astype(BF16)
    skip[...] = acc[4:6].astype(BF16)
    far[...] = acc[6:7].astype(BF16)


def backward(meta, tiles, same, other):
    return pl.pallas_call(
        backward_kernel,
        out_shape=(
            jax.ShapeDtypeStruct((2, TILE, FEAT), F32),
            jax.ShapeDtypeStruct((2, TILE, FEAT), BF16),
            jax.ShapeDtypeStruct((2, TILE, FEAT), BF16),
            jax.ShapeDtypeStruct((1, TILE, FEAT), BF16),
        ),
        in_specs=[SMEM_SPEC, VMEM_SPEC] + [ANY_SPEC] * 2,
        out_specs=(VMEM_SPEC,) * 4,
        scratch_shapes=[
            pltpu.VMEM((BANDS, TILE, FEAT), BF16),
            pltpu.VMEM((WINDOW, TILE, FEAT), F32),
            pltpu.SemaphoreType.DMA((2,)),
        ],
        compiler_params=params(),
        name="backward_tiles",
    )(meta, tiles, same, other)


def pair_kernel(parity, own, odd, skip, mine, sibling):
    p = parity[0]
    mine[...] = own[p] + odd[p].astype(F32) + skip[p].astype(F32)
    q = 1 - p
    sibling[...] = (own[q] + odd[q].astype(F32) + skip[q].astype(F32)).astype(BF16)


def pair_sum(parity, own, odd, skip):
    return pl.pallas_call(
        pair_kernel,
        out_shape=(
            jax.ShapeDtypeStruct((TILE, FEAT), F32),
            jax.ShapeDtypeStruct((TILE, FEAT), BF16),
        ),
        in_specs=[SMEM_SPEC] + [VMEM_SPEC] * 3,
        out_specs=(VMEM_SPEC,) * 2,
        compiler_params=params(),
        name="pair_sum",
    )(parity, own, odd, skip)


def summed(parts):
    total = parts[0].astype(F32)
    for i in range(1, parts.shape[0]):
        total = total + parts[i].astype(F32)
    return total


def middle_kernel(parts, out):
    total = summed(parts)
    bias = bias_rows(total[0:4, HALF:] + total[4:8, HALF:])
    row = jnp.concatenate([total[:, :HALF].astype(BF16), bias], axis=1)
    out[...] = jnp.broadcast_to(row[None], out.shape)


def middle_sum(parts, copies):
    return pl.pallas_call(
        middle_kernel,
        out_shape=jax.ShapeDtypeStruct((copies, 16, HALF + EXTRA), BF16),
        in_specs=[VMEM_SPEC],
        out_specs=VMEM_SPEC,
        compiler_params=params(),
        name="group_sum",
    )(parts)


def last_kernel(parts, out, bias_out):
    total = summed(parts)
    out[...] = jnp.broadcast_to(total[None, :, :HALF].astype(BF16), out.shape)
    bias = total[0:4, HALF:] + total[4:8, HALF:]
    for i in range(4):
        bias_out[:, i * 128 : (i + 1) * 128] = bias[i : i + 1]


def last_sum(parts, copies):
    return pl.pallas_call(
        last_kernel,
        out_shape=(
            jax.ShapeDtypeStruct((copies, 16, HALF), BF16),
            jax.ShapeDtypeStruct((1, FEAT), F32),
        ),
        in_specs=[VMEM_SPEC],
        out_specs=(VMEM_SPEC,) * 2,
        compiler_params=params(),
        name="total_sum",
    )(parts)


def join_kernel(core, mine, other, out):
    for k in range(2):

        @pl.when(core[0] == k)
        def _():
            out[:, k * HALF : (k + 1) * HALF] = mine[...].astype(F32)
            out[:, (1 - k) * HALF : (2 - k) * HALF] = other[...].astype(F32)


def join(core, mine, other):
    return pl.pallas_call(
        join_kernel,
        out_shape=jax.ShapeDtypeStruct((FEAT, FEAT), F32),
        in_specs=[SMEM_SPEC] + [VMEM_SPEC] * 2,
        out_specs=VMEM_SPEC,
        compiler_params=params(),
        name="join_halves",
    )(core, mine, other)


def after(value, other):
    return lax.optimization_barrier((value, other))[0]


def body(features, weight, bias_vec, tile_vals, tile_coords, tile_count, cotangent):
    own_row = lax.axis_index(ROW)
    core = lax.axis_index("core")
    parity = own_row & 1
    pair_row = own_row - parity
    tiles = stage(tile_vals[0, 0])
    coords = tile_coords[0, 0]
    block = coords[:, 0]
    block_at = (block & 1 ^ core) * (BANDS // 2) + (block >> 1)
    rel = coords[:, 1] - pair_row
    below = 2 + 2 * parity
    above = 4 - 2 * parity
    panel_at = jnp.where(
        (rel >= 0) & (rel < 2),
        rel,
        jnp.where(
            (rel >= -2) & (rel < 0),
            below + rel + 2,
            jnp.where((rel >= 2) & (rel < 4), above + rel - 2, 6),
        ),
    )
    meta = jnp.concatenate([block_at, panel_at, tile_count.reshape(1)])

    own = lax.all_gather(features, PAIR, axis=0, tiled=False)
    far = moved(features[None], to_far)
    odd = moved(own, to_odd)
    skip = moved(own, to_skip)
    mine, theirs = forward(meta, tiles, own, odd, skip, far)
    half = (mine + swapped(theirs).astype(F32)).astype(BF16)
    parts = exchange(half, "x")
    groups = lax.axis_size("y") * lax.axis_size("x")
    copies = lax.axis_size("z") * lax.axis_size("pair")
    side = core.reshape(1)
    layer_out, mids, w_mine, w_theirs = dense(
        side, parts, weight, bias_vec.reshape(1, FEAT), cotangent, groups
    )

    same = exchange(mids, "x")
    arrived = exchange(chip_sum(w_mine, swapped(w_theirs)), SPREAD)
    other = swapped(same)
    own_g, odd_g, skip_g, far_g = backward(meta, tiles, same, other)
    arrived = after(arrived, far_g)
    far_in = moved(far_g, to_far)
    odd_in = moved(odd_g, to_odd)
    skip_in = moved(skip_g, from_skip)
    keep, sibling = pair_sum(parity.reshape(1), own_g, odd_in, skip_in)
    sibling_in = moved(sibling, to_sibling)
    grad_features = (keep + far_in[0].astype(F32) + sibling_in.astype(F32)).astype(BF16)

    spread = middle_sum(arrived, copies)
    final, bias_total = last_sum(after(exchange(spread, REST), (odd_in, skip_in, far_in)), groups)
    w_half = exchange(final, SPREAD).reshape(FEAT, HALF)
    grad_weight = join(side, w_half, swapped(w_half))
    return (layer_out, grad_weight, bias_total.reshape(FEAT), grad_features)


def solution(mesh):
    split = Mesh(mesh.devices.reshape(8, 4, 2, 4, 2), ALL)
    return jax.shard_map(
        body,
        mesh=split,
        in_specs=(
            P(ALL, None),
            P(),
            P(),
            P(ROW, COL, None, None, None),
            P(ROW, COL, None, None),
            P(ROW, COL),
            P(ALL, None),
        ),
        out_specs=(P(ALL, None), P(), P(), P(ALL, None)),
        check_vma=False,
    )
```

```python
import jax
import jax.numpy as jnp
from jax import lax
from jax.experimental import pallas as pl
from jax.experimental.pallas import tpu as pltpu
from jax.sharding import Mesh, PartitionSpec as P

REACH = 3
WINDOW = 2 * REACH + 1
TILE = 128
FEAT = 512
BANDS = 8
SLOTS = 16
ROW = ("y", "z", "pair")
COL = ("x", "core")
ALL = ROW + COL
PAIR = "pair"
SPREAD = ("y", "x")
REST = ("z", "pair")
EXTRA = 128
HALF = 256
BF16 = jnp.bfloat16
F32 = jnp.float32
SQRT_2_OVER_PI = 0.7978845608028654
VMEM_LIMIT = 40 * 1024 * 1024

SMEM_SPEC = pl.BlockSpec(memory_space=pltpu.SMEM)
VMEM_SPEC = pl.BlockSpec(memory_space=pltpu.VMEM)
ANY_SPEC = pl.BlockSpec(memory_space=pl.ANY)
HBM_SPEC = pl.BlockSpec(memory_space=pltpu.HBM)


def params():
    return pltpu.CompilerParams(vmem_limit_bytes=VMEM_LIMIT)


def moved(block, target):
    size = lax.axis_size(ROW)
    return lax.ppermute(block, ROW, [(i, target(i) % size) for i in range(size)])


def to_sibling(i):
    return i ^ 1


def to_odd(i):
    return i + 1 if i % 2 else i - 1


def to_skip(i):
    return i + 2 if i % 2 else i - 2


def from_skip(i):
    return i - 2 if i % 2 else i + 2


def to_far(i):
    return i + 3 if i % 2 else i - 3


def swapped(block):
    return lax.ppermute(block, "core", [(0, 1), (1, 0)])


def exchange(chunks, axis):
    return lax.all_to_all(chunks, axis, 0, 0, tiled=True)


def copy_in(sources, targets, sems):
    copies = [
        pltpu.make_async_copy(s, t, sems.at[i]) for i, (s, t) in enumerate(zip(sources, targets))
    ]
    for c in copies:
        c.start()
    return copies


def stage_kernel(source, out, sem):
    copy = pltpu.make_async_copy(source, out, sem)
    copy.start()
    copy.wait()


def stage(tiles):
    return pl.pallas_call(
        stage_kernel,
        out_shape=jax.ShapeDtypeStruct(tiles.shape, tiles.dtype),
        in_specs=[HBM_SPEC],
        out_specs=VMEM_SPEC,
        scratch_shapes=[pltpu.SemaphoreType.DMA],
        compiler_params=params(),
        name="stage_tiles",
    )(tiles)


def for_live_slots(count, product, add):
    def four(g, carry):
        slots = [4 * g + i for i in range(4)]
        values = [product(s) for s in slots]
        for s, v in zip(slots, values):
            add(s, v)
        return carry

    def one(s, carry):
        add(s, product(s))
        return carry

    lax.fori_loop(0, count >> 2, four, 0)
    lax.fori_loop(count & ~3, count, one, 0)


def forward_kernel(meta, tiles, own, odd, skip, far, mine, theirs, panels, acc, sems):
    copies = copy_in(
        [own, odd, skip, far],
        [panels.at[0:2], panels.at[2:4], panels.at[4:6], panels.at[6:7]],
        sems,
    )
    acc[...] = jnp.zeros_like(acc)
    for c in copies:
        c.wait()

    def product(s):
        return jnp.dot(tiles[s], panels[meta[SLOTS + s]], preferred_element_type=F32)

    def add(s, value):
        acc[meta[s]] += value

    for_live_slots(meta[2 * SLOTS], product, add)
    mine[...] = acc[0:4]
    theirs[...] = acc[4:8].astype(BF16)


def forward(meta, tiles, own, odd, skip, far):
    return pl.pallas_call(
        forward_kernel,
        out_shape=(
            jax.ShapeDtypeStruct((BANDS // 2, TILE, FEAT), F32),
            jax.ShapeDtypeStruct((BANDS // 2, TILE, FEAT), BF16),
        ),
        in_specs=[SMEM_SPEC, VMEM_SPEC] + [ANY_SPEC] * 4,
        out_specs=(VMEM_SPEC,) * 2,
        scratch_shapes=[
            pltpu.VMEM((WINDOW, TILE, FEAT), BF16),
            pltpu.VMEM((BANDS, TILE, FEAT), F32),
            pltpu.SemaphoreType.DMA((4,)),
        ],
        compiler_params=params(),
        name="aggregate_tiles",
    )(meta, tiles, own, odd, skip, far)


def bias_rows(total):
    high = total.astype(BF16).astype(F32)
    return jnp.concatenate([high, total - high, jnp.zeros((8, 128), F32)], axis=0).astype(BF16)


def dense_kernel(core, parts, weight, bias, cot, layer_out, mids, mine, theirs, terms):
    agg = parts[0].astype(F32)
    for i in range(1, BANDS // 2):
        agg = agg + parts[i].astype(F32)
    agg_b = agg.astype(BF16)
    w = weight[...]
    v = jnp.dot(agg_b, w, preferred_element_type=F32) + bias[...]
    v2 = v * v
    t = jnp.tanh(SQRT_2_OVER_PI * (v + 0.044715 * (v2 * v)))
    half = 0.5 * (1.0 + t)
    layer_out[...] = (v * half).astype(BF16)
    slope = half + 0.5 * v * (1.0 - t * t) * (SQRT_2_OVER_PI * (1.0 + 3 * 0.044715 * v2))
    grad_pre = (cot[...].astype(F32) * slope).astype(BF16)
    mid = lax.dot_general(
        grad_pre, w, (((1,), (1,)), ((), ())), preferred_element_type=F32
    ).astype(BF16)
    mids[...] = jnp.broadcast_to(mid[None], mids.shape)
    term = lax.dot_general(agg_b, grad_pre, (((0,), (0,)), ((), ())), preferred_element_type=F32)
    count = mine.shape[0] - 1
    for i in range(2):
        terms[i] = term[:, i * HALF : (i + 1) * HALF].reshape(count, 16, HALF)
    k = core[0]
    mine[0:count] = terms[k]
    theirs[0:count] = terms[1 - k].astype(BF16)
    total = jnp.sum(grad_pre.astype(F32), axis=0, keepdims=True)
    total = jnp.concatenate([total[:, i * 128 : (i + 1) * 128] for i in range(4)], axis=0)
    zeros = jnp.zeros((16, HALF - EXTRA), F32)
    mine[count] = jnp.concatenate([bias_rows(total).astype(F32), zeros], axis=1)
    theirs[count] = jnp.concatenate([bias_rows(total), zeros.astype(BF16)], axis=1)


def dense(core, parts, weight, bias, cot, groups):
    return pl.pallas_call(
        dense_kernel,
        out_shape=(
            jax.ShapeDtypeStruct((TILE, FEAT), BF16),
            jax.ShapeDtypeStruct((BANDS // 2, TILE, FEAT), BF16),
            jax.ShapeDtypeStruct((groups + 1, 16, HALF), F32),
            jax.ShapeDtypeStruct((groups + 1, 16, HALF), BF16),
        ),
        in_specs=[SMEM_SPEC] + [VMEM_SPEC] * 4,
        out_specs=(VMEM_SPEC,) * 4,
        scratch_shapes=[pltpu.VMEM((2, groups, 16, HALF), F32)],
        compiler_params=params(),
        name="dense_layer",
    )(core, parts, weight, bias, cot)


def chip_kernel(mine, theirs, out):
    count = out.shape[0]
    out[:, :, :HALF] = (mine[0:count] + theirs[0:count].astype(F32)).astype(BF16)
    both = mine[count, :, :EXTRA] + theirs[count, :, :EXTRA].astype(F32)
    bias = bias_rows(both[0:4] + both[4:8])
    out[:, :, HALF:] = jnp.broadcast_to(bias[None], (count, 16, EXTRA))


def chip_sum(mine, theirs):
    count = mine.shape[0] - 1
    return pl.pallas_call(
        chip_kernel,
        out_shape=jax.ShapeDtypeStruct((count, 16, HALF + EXTRA), BF16),
        in_specs=[VMEM_SPEC] * 2,
        out_specs=VMEM_SPEC,
        compiler_params=params(),
        name="chip_sum",
    )(mine, theirs)


def backward_kernel(meta, tiles, same, other, own, odd, skip, panels, acc, sems):
    copies = copy_in([same, other], [panels.at[0:4], panels.at[4:8]], sems)
    acc[...] = jnp.zeros_like(acc)
    for c in copies:
        c.wait()

    def product(s):
        return lax.dot_general(
            tiles[s], panels[meta[s]], (((0,), (0,)), ((), ())), preferred_element_type=F32
        )

    def add(s, value):
        acc[meta[SLOTS + s]] += value

    for_live_slots(meta[2 * SLOTS], product, add)
    own[...] = acc[0:2]
    odd[0:2] = acc[2:4].astype(BF16)
    odd[2:3] = acc[6:7].astype(BF16)
    skip[...] = acc[4:6]


def backward(meta, tiles, same, other):
    return pl.pallas_call(
        backward_kernel,
        out_shape=(
            jax.ShapeDtypeStruct((2, TILE, FEAT), F32),
            jax.ShapeDtypeStruct((3, TILE, FEAT), BF16),
            jax.ShapeDtypeStruct((2, TILE, FEAT), F32),
        ),
        in_specs=[SMEM_SPEC, VMEM_SPEC] + [ANY_SPEC] * 2,
        out_specs=(VMEM_SPEC,) * 3,
        scratch_shapes=[
            pltpu.VMEM((BANDS, TILE, FEAT), BF16),
            pltpu.VMEM((WINDOW, TILE, FEAT), F32),
            pltpu.SemaphoreType.DMA((2,)),
        ],
        compiler_params=params(),
        name="backward_tiles",
    )(meta, tiles, same, other)


def relay_kernel(parity, skip, odd, out):
    p = parity[0]
    q = 1 - p
    out[p] = (skip[p] + odd[2].astype(F32)).astype(BF16)
    out[q] = skip[q].astype(BF16)


def relay_sum(parity, skip, odd):
    return pl.pallas_call(
        relay_kernel,
        out_shape=jax.ShapeDtypeStruct((2, TILE, FEAT), BF16),
        in_specs=[SMEM_SPEC] + [VMEM_SPEC] * 2,
        out_specs=VMEM_SPEC,
        compiler_params=params(),
        name="relay_sum",
    )(parity, skip, odd)


def pair_kernel(parity, own, odd, skip, mine, sibling):
    p = parity[0]
    mine[...] = own[p] + odd[p].astype(F32) + skip[p].astype(F32)
    q = 1 - p
    sibling[...] = (own[q] + odd[q].astype(F32) + skip[q].astype(F32)).astype(BF16)


def pair_sum(parity, own, odd, skip):
    return pl.pallas_call(
        pair_kernel,
        out_shape=(
            jax.ShapeDtypeStruct((TILE, FEAT), F32),
            jax.ShapeDtypeStruct((TILE, FEAT), BF16),
        ),
        in_specs=[SMEM_SPEC] + [VMEM_SPEC] * 3,
        out_specs=(VMEM_SPEC,) * 2,
        compiler_params=params(),
        name="pair_sum",
    )(parity, own, odd, skip)


def summed(parts):
    total = parts[0].astype(F32)
    for i in range(1, parts.shape[0]):
        total = total + parts[i].astype(F32)
    return total


def middle_kernel(parts, out):
    total = summed(parts)
    bias = bias_rows(total[0:4, HALF:] + total[4:8, HALF:])
    row = jnp.concatenate([total[:, :HALF].astype(BF16), bias], axis=1)
    out[...] = jnp.broadcast_to(row[None], out.shape)


def middle_sum(parts, copies):
    return pl.pallas_call(
        middle_kernel,
        out_shape=jax.ShapeDtypeStruct((copies, 16, HALF + EXTRA), BF16),
        in_specs=[VMEM_SPEC],
        out_specs=VMEM_SPEC,
        compiler_params=params(),
        name="group_sum",
    )(parts)


def last_kernel(parts, out, bias_out):
    total = summed(parts)
    out[...] = jnp.broadcast_to(total[None, :, :HALF].astype(BF16), out.shape)
    bias = total[0:4, HALF:] + total[4:8, HALF:]
    for i in range(4):
        bias_out[:, i * 128 : (i + 1) * 128] = bias[i : i + 1]


def last_sum(parts, copies):
    return pl.pallas_call(
        last_kernel,
        out_shape=(
            jax.ShapeDtypeStruct((copies, 16, HALF), BF16),
            jax.ShapeDtypeStruct((1, FEAT), F32),
        ),
        in_specs=[VMEM_SPEC],
        out_specs=(VMEM_SPEC,) * 2,
        compiler_params=params(),
        name="total_sum",
    )(parts)


def join_kernel(core, mine, other, out):
    for k in range(2):

        @pl.when(core[0] == k)
        def _():
            out[:, k * HALF : (k + 1) * HALF] = mine[...].astype(F32)
            out[:, (1 - k) * HALF : (2 - k) * HALF] = other[...].astype(F32)


def join(core, mine, other):
    return pl.pallas_call(
        join_kernel,
        out_shape=jax.ShapeDtypeStruct((FEAT, FEAT), F32),
        in_specs=[SMEM_SPEC] + [VMEM_SPEC] * 2,
        out_specs=VMEM_SPEC,
        compiler_params=params(),
        name="join_halves",
    )(core, mine, other)


def after(value, other):
    return lax.optimization_barrier((value, other))[0]


def body(features, weight, bias_vec, tile_vals, tile_coords, tile_count, cotangent):
    own_row = lax.axis_index(ROW)
    core = lax.axis_index("core")
    parity = own_row & 1
    pair_row = own_row - parity
    tiles = stage(tile_vals[0, 0])
    coords = tile_coords[0, 0]
    block = coords[:, 0]
    block_at = (block & 1 ^ core) * (BANDS // 2) + (block >> 1)
    rel = coords[:, 1] - pair_row
    below = 2 + 2 * parity
    above = 4 - 2 * parity
    panel_at = jnp.where(
        (rel >= 0) & (rel < 2),
        rel,
        jnp.where(
            (rel >= -2) & (rel < 0),
            below + rel + 2,
            jnp.where((rel >= 2) & (rel < 4), above + rel - 2, 6),
        ),
    )
    meta = jnp.concatenate([block_at, panel_at, tile_count.reshape(1)])

    own = lax.all_gather(features, PAIR, axis=0, tiled=False)
    far = moved(features[None], to_far)
    odd = moved(own, to_odd)
    skip = moved(own, to_skip)
    mine, theirs = forward(meta, tiles, own, odd, skip, far)
    half = (mine + swapped(theirs).astype(F32)).astype(BF16)
    parts = exchange(half, "x")
    groups = lax.axis_size("y") * lax.axis_size("x")
    copies = lax.axis_size("z") * lax.axis_size("pair")
    side = core.reshape(1)
    layer_out, mids, w_mine, w_theirs = dense(
        side, parts, weight, bias_vec.reshape(1, FEAT), cotangent, groups
    )

    same = exchange(mids, "x")
    arrived = exchange(chip_sum(w_mine, swapped(w_theirs)), SPREAD)
    other = swapped(same)
    own_g, odd_g, skip_g = backward(meta, tiles, same, other)
    arrived = after(arrived, odd_g)
    side_row = parity.reshape(1)
    odd_in = moved(odd_g, to_odd)
    skip_out = relay_sum(side_row, skip_g, odd_in)
    skip_in = moved(skip_out, from_skip)
    keep, sibling = pair_sum(side_row, own_g, odd_in, skip_in)
    grad_features = (keep + moved(sibling, to_sibling).astype(F32)).astype(BF16)

    spread = middle_sum(arrived, copies)
    summed_in = after(exchange(spread, REST), skip_out)
    final, bias_total = last_sum(summed_in, groups)
    w_half = exchange(final, SPREAD).reshape(FEAT, HALF)
    grad_weight = join(side, w_half, swapped(w_half))
    return (layer_out, grad_weight, bias_total.reshape(FEAT), grad_features)


def solution(mesh):
    split = Mesh(mesh.devices.reshape(8, 4, 2, 4, 2), ALL)
    return jax.shard_map(
        body,
        mesh=split,
        in_specs=(
            P(ALL, None),
            P(),
            P(),
            P(ROW, COL, None, None, None),
            P(ROW, COL, None, None),
            P(ROW, COL),
            P(ALL, None),
        ),
        out_specs=(P(ALL, None), P(), P(), P(ALL, None)),
        check_vma=False,
    )
```

```python
import jax
import jax.numpy as jnp
from jax import lax
from jax.experimental import pallas as pl
from jax.experimental.pallas import tpu as pltpu
from jax.sharding import Mesh, PartitionSpec as P

REACH = 3
WINDOW = 2 * REACH + 1
TILE = 128
FEAT = 512
BANDS = 8
SLOTS = 16
ROW = ("y", "z", "pair")
COL = ("x", "core")
ALL = ROW + COL
PAIR = "pair"
SPREAD = ("z", "pair", "x")
REST = ("y",)
EXTRA = 128
HALF = 256
BF16 = jnp.bfloat16
F32 = jnp.float32
SQRT_2_OVER_PI = 0.7978845608028654
VMEM_LIMIT = 40 * 1024 * 1024

SMEM_SPEC = pl.BlockSpec(memory_space=pltpu.SMEM)
VMEM_SPEC = pl.BlockSpec(memory_space=pltpu.VMEM)
ANY_SPEC = pl.BlockSpec(memory_space=pl.ANY)
HBM_SPEC = pl.BlockSpec(memory_space=pltpu.HBM)


def params():
    return pltpu.CompilerParams(vmem_limit_bytes=VMEM_LIMIT)


def moved(block, target):
    size = lax.axis_size(ROW)
    return lax.ppermute(block, ROW, [(i, target(i) % size) for i in range(size)])


def to_sibling(i):
    return i ^ 1


def to_odd(i):
    return i + 1 if i % 2 else i - 1


def to_skip(i):
    return i + 2 if i % 2 else i - 2


def from_skip(i):
    return i - 2 if i % 2 else i + 2


def to_far(i):
    return i + 3 if i % 2 else i - 3


def swapped(block):
    return lax.ppermute(block, "core", [(0, 1), (1, 0)])


def exchange(chunks, axis):
    return lax.all_to_all(chunks, axis, 0, 0, tiled=True)


def copy_in(sources, targets, sems):
    copies = [
        pltpu.make_async_copy(s, t, sems.at[i]) for i, (s, t) in enumerate(zip(sources, targets))
    ]
    for c in copies:
        c.start()
    return copies


def stage_kernel(tiles, bias, tiles_out, bias_out, sems):
    for c in copy_in([tiles, bias], [tiles_out, bias_out], sems):
        c.wait()


def stage(tiles, bias):
    return pl.pallas_call(
        stage_kernel,
        out_shape=(
            jax.ShapeDtypeStruct(tiles.shape, tiles.dtype),
            jax.ShapeDtypeStruct(bias.shape, bias.dtype),
        ),
        in_specs=[HBM_SPEC] * 2,
        out_specs=(VMEM_SPEC,) * 2,
        scratch_shapes=[pltpu.SemaphoreType.DMA((2,))],
        compiler_params=params(),
        name="stage_tiles",
    )(tiles, bias)


def for_live_slots(count, product, add):
    def four(g, carry):
        slots = [4 * g + i for i in range(4)]
        values = [product(s) for s in slots]
        for s, v in zip(slots, values):
            add(s, v)
        return carry

    def one(s, carry):
        add(s, product(s))
        return carry

    lax.fori_loop(0, count >> 2, four, 0)
    lax.fori_loop(count & ~3, count, one, 0)


def bundle_kernel(parity, own, skip, out):
    out[0:2] = own[...]
    out[2] = skip[parity[0]]


def bundle(parity, own, skip):
    return pl.pallas_call(
        bundle_kernel,
        out_shape=jax.ShapeDtypeStruct((3, TILE, FEAT), BF16),
        in_specs=[SMEM_SPEC] + [VMEM_SPEC] * 2,
        out_specs=VMEM_SPEC,
        compiler_params=params(),
        name="bundle_panels",
    )(parity, own, skip)


def forward_kernel(meta, tiles, own, odd, skip, mine, theirs, panels, acc, sems):
    copies = copy_in(
        [own, odd.at[0:2], skip, odd.at[2:3]],
        [panels.at[0:2], panels.at[2:4], panels.at[4:6], panels.at[6:7]],
        sems,
    )
    acc[...] = jnp.zeros_like(acc)
    for c in copies:
        c.wait()

    def product(s):
        return jnp.dot(tiles[s], panels[meta[SLOTS + s]], preferred_element_type=F32)

    def add(s, value):
        acc[meta[s]] += value

    for_live_slots(meta[2 * SLOTS], product, add)
    mine[...] = acc[0:4]
    theirs[...] = acc[4:8].astype(BF16)


def forward(meta, tiles, own, odd, skip):
    return pl.pallas_call(
        forward_kernel,
        out_shape=(
            jax.ShapeDtypeStruct((BANDS // 2, TILE, FEAT), F32),
            jax.ShapeDtypeStruct((BANDS // 2, TILE, FEAT), BF16),
        ),
        in_specs=[SMEM_SPEC, VMEM_SPEC] + [ANY_SPEC] * 3,
        out_specs=(VMEM_SPEC,) * 2,
        scratch_shapes=[
            pltpu.VMEM((WINDOW, TILE, FEAT), BF16),
            pltpu.VMEM((BANDS, TILE, FEAT), F32),
            pltpu.SemaphoreType.DMA((4,)),
        ],
        compiler_params=params(),
        name="aggregate_tiles",
    )(meta, tiles, own, odd, skip)


def bias_rows(total):
    high = total.astype(BF16).astype(F32)
    return jnp.concatenate([high, total - high, jnp.zeros((8, 128), F32)], axis=0).astype(BF16)


def dense_kernel(core, parts, weight, bias, cot, layer_out, mids, mine, theirs, terms):
    agg = parts[0].astype(F32)
    for i in range(1, BANDS // 2):
        agg = agg + parts[i].astype(F32)
    agg_b = agg.astype(BF16)
    w = weight[...]
    v = jnp.dot(agg_b, w, preferred_element_type=F32) + bias[...]
    v2 = v * v
    t = jnp.tanh(SQRT_2_OVER_PI * (v + 0.044715 * (v2 * v)))
    half = 0.5 * (1.0 + t)
    layer_out[...] = (v * half).astype(BF16)
    slope = half + 0.5 * v * (1.0 - t * t) * (SQRT_2_OVER_PI * (1.0 + 3 * 0.044715 * v2))
    grad_pre = (cot[...].astype(F32) * slope).astype(BF16)
    mid = lax.dot_general(
        grad_pre, w, (((1,), (1,)), ((), ())), preferred_element_type=F32
    ).astype(BF16)
    mids[...] = jnp.broadcast_to(mid[None], mids.shape)
    term = lax.dot_general(agg_b, grad_pre, (((0,), (0,)), ((), ())), preferred_element_type=F32)
    count = mine.shape[0] - 1
    for i in range(2):
        terms[i] = term[:, i * HALF : (i + 1) * HALF].reshape(count, 16, HALF)
    k = core[0]
    mine[0:count] = terms[k]
    theirs[0:count] = terms[1 - k].astype(BF16)
    total = jnp.sum(grad_pre.astype(F32), axis=0, keepdims=True)
    total = jnp.concatenate([total[:, i * 128 : (i + 1) * 128] for i in range(4)], axis=0)
    zeros = jnp.zeros((16, HALF - EXTRA), F32)
    mine[count] = jnp.concatenate([bias_rows(total).astype(F32), zeros], axis=1)
    theirs[count] = jnp.concatenate([bias_rows(total), zeros.astype(BF16)], axis=1)


def dense(core, parts, weight, bias, cot, groups):
    return pl.pallas_call(
        dense_kernel,
        out_shape=(
            jax.ShapeDtypeStruct((TILE, FEAT), BF16),
            jax.ShapeDtypeStruct((BANDS // 2, TILE, FEAT), BF16),
            jax.ShapeDtypeStruct((groups + 1, 16, HALF), F32),
            jax.ShapeDtypeStruct((groups + 1, 16, HALF), BF16),
        ),
        in_specs=[SMEM_SPEC] + [VMEM_SPEC] * 4,
        out_specs=(VMEM_SPEC,) * 4,
        scratch_shapes=[pltpu.VMEM((2, groups, 16, HALF), F32)],
        compiler_params=params(),
        name="dense_layer",
    )(core, parts, weight, bias, cot)


def chip_kernel(mine, theirs, out):
    count = out.shape[0]
    out[:, :, :HALF] = (mine[0:count] + theirs[0:count].astype(F32)).astype(BF16)
    both = mine[count, :, :EXTRA] + theirs[count, :, :EXTRA].astype(F32)
    bias = bias_rows(both[0:4] + both[4:8])
    out[:, :, HALF:] = jnp.broadcast_to(bias[None], (count, 16, EXTRA))


def chip_sum(mine, theirs):
    count = mine.shape[0] - 1
    return pl.pallas_call(
        chip_kernel,
        out_shape=jax.ShapeDtypeStruct((count, 16, HALF + EXTRA), BF16),
        in_specs=[VMEM_SPEC] * 2,
        out_specs=VMEM_SPEC,
        compiler_params=params(),
        name="chip_sum",
    )(mine, theirs)


def backward_kernel(meta, tiles, same, other, own, odd, skip, panels, acc, sems):
    copies = copy_in([same, other], [panels.at[0:4], panels.at[4:8]], sems)
    acc[...] = jnp.zeros_like(acc)
    for c in copies:
        c.wait()

    def product(s):
        return lax.dot_general(
            tiles[s], panels[meta[s]], (((0,), (0,)), ((), ())), preferred_element_type=F32
        )

    def add(s, value):
        acc[meta[SLOTS + s]] += value

    for_live_slots(meta[2 * SLOTS], product, add)
    own[...] = acc[0:2]
    odd[0:2] = acc[2:4].astype(BF16)
    odd[2:3] = acc[6:7].astype(BF16)
    skip[...] = acc[4:6]


def backward(meta, tiles, same, other):
    return pl.pallas_call(
        backward_kernel,
        out_shape=(
            jax.ShapeDtypeStruct((2, TILE, FEAT), F32),
            jax.ShapeDtypeStruct((3, TILE, FEAT), BF16),
            jax.ShapeDtypeStruct((2, TILE, FEAT), F32),
        ),
        in_specs=[SMEM_SPEC, VMEM_SPEC] + [ANY_SPEC] * 2,
        out_specs=(VMEM_SPEC,) * 3,
        scratch_shapes=[
            pltpu.VMEM((BANDS, TILE, FEAT), BF16),
            pltpu.VMEM((WINDOW, TILE, FEAT), F32),
            pltpu.SemaphoreType.DMA((2,)),
        ],
        compiler_params=params(),
        name="backward_tiles",
    )(meta, tiles, same, other)


def relay_kernel(parity, skip, odd, out):
    p = parity[0]
    q = 1 - p
    out[p] = (skip[p] + odd[2].astype(F32)).astype(BF16)
    out[q] = skip[q].astype(BF16)


def relay_sum(parity, skip, odd):
    return pl.pallas_call(
        relay_kernel,
        out_shape=jax.ShapeDtypeStruct((2, TILE, FEAT), BF16),
        in_specs=[SMEM_SPEC] + [VMEM_SPEC] * 2,
        out_specs=VMEM_SPEC,
        compiler_params=params(),
        name="relay_sum",
    )(parity, skip, odd)


def pair_kernel(parity, own, odd, skip, mine, sibling):
    p = parity[0]
    mine[...] = own[p] + odd[p].astype(F32) + skip[p].astype(F32)
    q = 1 - p
    sibling[...] = (own[q] + odd[q].astype(F32) + skip[q].astype(F32)).astype(BF16)


def pair_sum(parity, own, odd, skip):
    return pl.pallas_call(
        pair_kernel,
        out_shape=(
            jax.ShapeDtypeStruct((TILE, FEAT), F32),
            jax.ShapeDtypeStruct((TILE, FEAT), BF16),
        ),
        in_specs=[SMEM_SPEC] + [VMEM_SPEC] * 3,
        out_specs=(VMEM_SPEC,) * 2,
        compiler_params=params(),
        name="pair_sum",
    )(parity, own, odd, skip)


def summed(parts):
    total = parts[0].astype(F32)
    for i in range(1, parts.shape[0]):
        total = total + parts[i].astype(F32)
    return total


def middle_kernel(parts, out):
    total = summed(parts)
    bias = bias_rows(total[0:4, HALF:] + total[4:8, HALF:])
    row = jnp.concatenate([total[:, :HALF].astype(BF16), bias], axis=1)
    out[...] = jnp.broadcast_to(row[None], out.shape)


def middle_sum(parts, copies):
    return pl.pallas_call(
        middle_kernel,
        out_shape=jax.ShapeDtypeStruct((copies, 16, HALF + EXTRA), BF16),
        in_specs=[VMEM_SPEC],
        out_specs=VMEM_SPEC,
        compiler_params=params(),
        name="group_sum",
    )(parts)


def last_kernel(parts, out, bias_out):
    total = summed(parts)
    out[...] = jnp.broadcast_to(total[None, :, :HALF].astype(BF16), out.shape)
    bias = total[0:4, HALF:] + total[4:8, HALF:]
    for i in range(4):
        bias_out[:, i * 128 : (i + 1) * 128] = bias[i : i + 1]


def last_sum(parts, copies):
    return pl.pallas_call(
        last_kernel,
        out_shape=(
            jax.ShapeDtypeStruct((copies, 16, HALF), BF16),
            jax.ShapeDtypeStruct((1, FEAT), F32),
        ),
        in_specs=[VMEM_SPEC],
        out_specs=(VMEM_SPEC,) * 2,
        compiler_params=params(),
        name="total_sum",
    )(parts)


def join_kernel(core, mine, other, out):
    for k in range(2):

        @pl.when(core[0] == k)
        def _():
            out[:, k * HALF : (k + 1) * HALF] = mine[...].astype(F32)
            out[:, (1 - k) * HALF : (2 - k) * HALF] = other[...].astype(F32)


def join(core, mine, other):
    return pl.pallas_call(
        join_kernel,
        out_shape=jax.ShapeDtypeStruct((FEAT, FEAT), F32),
        in_specs=[SMEM_SPEC] + [VMEM_SPEC] * 2,
        out_specs=VMEM_SPEC,
        compiler_params=params(),
        name="join_halves",
    )(core, mine, other)


def after(value, other):
    return lax.optimization_barrier((value, other))[0]


def body(features, weight, bias_vec, tile_vals, tile_coords, tile_count, cotangent):
    own_row = lax.axis_index(ROW)
    core = lax.axis_index("core")
    parity = own_row & 1
    pair_row = own_row - parity
    tiles, bias = stage(tile_vals[0, 0], bias_vec.reshape(1, FEAT))
    coords = tile_coords[0, 0]
    block = coords[:, 0]
    block_at = (block & 1 ^ core) * (BANDS // 2) + (block >> 1)
    rel = coords[:, 1] - pair_row
    below = 2 + 2 * parity
    above = 4 - 2 * parity
    panel_at = jnp.where(
        (rel >= 0) & (rel < 2),
        rel,
        jnp.where(
            (rel >= -2) & (rel < 0),
            below + rel + 2,
            jnp.where((rel >= 2) & (rel < 4), above + rel - 2, 6),
        ),
    )
    meta = jnp.concatenate([block_at, panel_at, tile_count.reshape(1)])

    own = lax.all_gather(features, PAIR, axis=0, tiled=False)
    side_row = parity.reshape(1)
    skip = moved(own, to_skip)
    odd = moved(bundle(side_row, own, skip), to_odd)
    mine, theirs = forward(meta, tiles, own, odd, skip)
    half = (mine + swapped(theirs).astype(F32)).astype(BF16)
    parts = exchange(half, "x")
    groups = lax.axis_size(SPREAD)
    copies = lax.axis_size(REST)
    side = core.reshape(1)
    layer_out, mids, w_mine, w_theirs = dense(
        side, parts, weight, bias, cotangent, groups
    )

    same = exchange(mids, "x")
    arrived = exchange(chip_sum(w_mine, swapped(w_theirs)), SPREAD)
    other = swapped(same)
    own_g, odd_g, skip_g = backward(meta, tiles, same, other)
    arrived = after(arrived, odd_g)
    odd_in = moved(odd_g, to_odd)
    skip_out = relay_sum(side_row, skip_g, odd_in)
    skip_in = moved(skip_out, from_skip)
    keep, sibling = pair_sum(side_row, own_g, odd_in, skip_in)
    grad_features = (keep + moved(sibling, to_sibling).astype(F32)).astype(BF16)

    spread = middle_sum(arrived, copies)
    summed_in = after(exchange(spread, REST), skip_out)
    final, bias_total = last_sum(summed_in, groups)
    w_half = exchange(final, SPREAD).reshape(FEAT, HALF)
    grad_weight = join(side, w_half, swapped(w_half))
    return (layer_out, grad_weight, bias_total.reshape(FEAT), grad_features)


def solution(mesh):
    split = Mesh(mesh.devices.reshape(8, 4, 2, 4, 2), ALL)
    return jax.shard_map(
        body,
        mesh=split,
        in_specs=(
            P(ALL, None),
            P(),
            P(),
            P(ROW, COL, None, None, None),
            P(ROW, COL, None, None),
            P(ROW, COL),
            P(ALL, None),
        ),
        out_specs=(P(ALL, None), P(), P(), P(ALL, None)),
        check_vma=False,
    )
```

```python
import jax
import jax.numpy as jnp
from jax import lax
from jax.experimental import pallas as pl
from jax.experimental.pallas import tpu as pltpu
from jax.sharding import Mesh, PartitionSpec as P

REACH = 3
WINDOW = 2 * REACH + 1
TILE = 128
FEAT = 512
BANDS = 8
SLOTS = 16
ROW = ("y", "z", "pair")
COL = ("x", "core")
ALL = ROW + COL
PAIR = "pair"
SPREAD = ("z", "pair", "x")
REST = ("y",)
EXTRA = 128
HALF = 256
BF16 = jnp.bfloat16
F32 = jnp.float32
SQRT_2_OVER_PI = 0.7978845608028654
VMEM_LIMIT = 40 * 1024 * 1024

SMEM_SPEC = pl.BlockSpec(memory_space=pltpu.SMEM)
VMEM_SPEC = pl.BlockSpec(memory_space=pltpu.VMEM)
ANY_SPEC = pl.BlockSpec(memory_space=pl.ANY)
HBM_SPEC = pl.BlockSpec(memory_space=pltpu.HBM)


def params():
    return pltpu.CompilerParams(vmem_limit_bytes=VMEM_LIMIT)


def moved(block, target):
    size = lax.axis_size(ROW)
    return lax.ppermute(block, ROW, [(i, target(i) % size) for i in range(size)])


def to_sibling(i):
    return i ^ 1


def to_odd(i):
    return i + 1 if i % 2 else i - 1


def to_skip(i):
    return i + 2 if i % 2 else i - 2


def from_skip(i):
    return i - 2 if i % 2 else i + 2


def to_far(i):
    return i + 3 if i % 2 else i - 3


def swapped(block):
    return lax.ppermute(block, "core", [(0, 1), (1, 0)])


def exchange(chunks, axis):
    return lax.all_to_all(chunks, axis, 0, 0, tiled=True)


def copy_in(sources, targets, sems):
    copies = [
        pltpu.make_async_copy(s, t, sems.at[i]) for i, (s, t) in enumerate(zip(sources, targets))
    ]
    for c in copies:
        c.start()
    return copies


def stage_kernel(tiles, bias, tiles_out, bias_out, sems):
    for c in copy_in([tiles, bias], [tiles_out, bias_out], sems):
        c.wait()


def stage(tiles, bias):
    return pl.pallas_call(
        stage_kernel,
        out_shape=(
            jax.ShapeDtypeStruct(tiles.shape, tiles.dtype),
            jax.ShapeDtypeStruct(bias.shape, bias.dtype),
        ),
        in_specs=[HBM_SPEC] * 2,
        out_specs=(VMEM_SPEC,) * 2,
        scratch_shapes=[pltpu.SemaphoreType.DMA((2,))],
        compiler_params=params(),
        name="stage_tiles",
    )(tiles, bias)


def for_live_slots(count, product, add):
    def four(g, carry):
        slots = [4 * g + i for i in range(4)]
        values = [product(s) for s in slots]
        for s, v in zip(slots, values):
            add(s, v)
        return carry

    def one(s, carry):
        add(s, product(s))
        return carry

    lax.fori_loop(0, count >> 2, four, 0)
    lax.fori_loop(count & ~3, count, one, 0)


def pick_kernel(parity, skip, out):
    out[0] = skip[parity[0]]


def pick(parity, skip):
    return pl.pallas_call(
        pick_kernel,
        out_shape=jax.ShapeDtypeStruct((1, TILE, FEAT), BF16),
        in_specs=[SMEM_SPEC, VMEM_SPEC],
        out_specs=VMEM_SPEC,
        compiler_params=params(),
        name="pick_panel",
    )(parity, skip)


def forward_kernel(meta, tiles, own, odd, skip, far, mine, theirs, panels, acc, sems):
    copies = copy_in(
        [own, odd, skip, far],
        [panels.at[0:2], panels.at[2:4], panels.at[4:6], panels.at[6:7]],
        sems,
    )
    acc[...] = jnp.zeros_like(acc)
    for c in copies:
        c.wait()

    def product(s):
        return jnp.dot(tiles[s], panels[meta[SLOTS + s]], preferred_element_type=F32)

    def add(s, value):
        acc[meta[s]] += value

    for_live_slots(meta[2 * SLOTS], product, add)
    mine[...] = acc[0:4]
    theirs[...] = acc[4:8].astype(BF16)


def forward(meta, tiles, own, odd, skip, far):
    return pl.pallas_call(
        forward_kernel,
        out_shape=(
            jax.ShapeDtypeStruct((BANDS // 2, TILE, FEAT), F32),
            jax.ShapeDtypeStruct((BANDS // 2, TILE, FEAT), BF16),
        ),
        in_specs=[SMEM_SPEC, VMEM_SPEC] + [ANY_SPEC] * 4,
        out_specs=(VMEM_SPEC,) * 2,
        scratch_shapes=[
            pltpu.VMEM((WINDOW, TILE, FEAT), BF16),
            pltpu.VMEM((BANDS, TILE, FEAT), F32),
            pltpu.SemaphoreType.DMA((4,)),
        ],
        compiler_params=params(),
        name="aggregate_tiles",
    )(meta, tiles, own, odd, skip, far)


def bias_rows(total):
    high = total.astype(BF16).astype(F32)
    return jnp.concatenate([high, total - high, jnp.zeros((8, 128), F32)], axis=0).astype(BF16)


def dense_kernel(core, parts, weight, bias, cot, layer_out, mids, mine, theirs, terms):
    agg = parts[0].astype(F32)
    for i in range(1, BANDS // 2):
        agg = agg + parts[i].astype(F32)
    agg_b = agg.astype(BF16)
    w = weight[...]
    v = jnp.dot(agg_b, w, preferred_element_type=F32) + bias[...]
    v2 = v * v
    t = jnp.tanh(SQRT_2_OVER_PI * (v + 0.044715 * (v2 * v)))
    half = 0.5 * (1.0 + t)
    layer_out[...] = (v * half).astype(BF16)
    slope = half + 0.5 * v * (1.0 - t * t) * (SQRT_2_OVER_PI * (1.0 + 3 * 0.044715 * v2))
    grad_pre = (cot[...].astype(F32) * slope).astype(BF16)
    mid = lax.dot_general(
        grad_pre, w, (((1,), (1,)), ((), ())), preferred_element_type=F32
    ).astype(BF16)
    mids[...] = jnp.broadcast_to(mid[None], mids.shape)
    term = lax.dot_general(agg_b, grad_pre, (((0,), (0,)), ((), ())), preferred_element_type=F32)
    count = mine.shape[0] - 1
    for i in range(2):
        terms[i] = term[:, i * HALF : (i + 1) * HALF].reshape(count, 16, HALF)
    k = core[0]
    mine[0:count] = terms[k]
    theirs[0:count] = terms[1 - k].astype(BF16)
    total = jnp.sum(grad_pre.astype(F32), axis=0, keepdims=True)
    total = jnp.concatenate([total[:, i * 128 : (i + 1) * 128] for i in range(4)], axis=0)
    zeros = jnp.zeros((16, HALF - EXTRA), F32)
    mine[count] = jnp.concatenate([bias_rows(total).astype(F32), zeros], axis=1)
    theirs[count] = jnp.concatenate([bias_rows(total), zeros.astype(BF16)], axis=1)


def dense(core, parts, weight, bias, cot, groups):
    return pl.pallas_call(
        dense_kernel,
        out_shape=(
            jax.ShapeDtypeStruct((TILE, FEAT), BF16),
            jax.ShapeDtypeStruct((BANDS // 2, TILE, FEAT), BF16),
            jax.ShapeDtypeStruct((groups + 1, 16, HALF), F32),
            jax.ShapeDtypeStruct((groups + 1, 16, HALF), BF16),
        ),
        in_specs=[SMEM_SPEC] + [VMEM_SPEC] * 4,
        out_specs=(VMEM_SPEC,) * 4,
        scratch_shapes=[pltpu.VMEM((2, groups, 16, HALF), F32)],
        compiler_params=params(),
        name="dense_layer",
    )(core, parts, weight, bias, cot)


def chip_kernel(mine, theirs, out):
    count = out.shape[0]
    out[:, :, :HALF] = (mine[0:count] + theirs[0:count].astype(F32)).astype(BF16)
    both = mine[count, :, :EXTRA] + theirs[count, :, :EXTRA].astype(F32)
    bias = bias_rows(both[0:4] + both[4:8])
    out[:, :, HALF:] = jnp.broadcast_to(bias[None], (count, 16, EXTRA))


def chip_sum(mine, theirs):
    count = mine.shape[0] - 1
    return pl.pallas_call(
        chip_kernel,
        out_shape=jax.ShapeDtypeStruct((count, 16, HALF + EXTRA), BF16),
        in_specs=[VMEM_SPEC] * 2,
        out_specs=VMEM_SPEC,
        compiler_params=params(),
        name="chip_sum",
    )(mine, theirs)


def backward_kernel(meta, tiles, same, other, own, odd, skip, panels, acc, sems):
    copies = copy_in([same, other], [panels.at[0:4], panels.at[4:8]], sems)
    acc[...] = jnp.zeros_like(acc)
    for c in copies:
        c.wait()

    def product(s):
        return lax.dot_general(
            tiles[s], panels[meta[s]], (((0,), (0,)), ((), ())), preferred_element_type=F32
        )

    def add(s, value):
        acc[meta[SLOTS + s]] += value

    for_live_slots(meta[2 * SLOTS], product, add)
    own[...] = acc[0:2]
    odd[0:2] = acc[2:4].astype(BF16)
    odd[2:3] = acc[6:7].astype(BF16)
    skip[...] = acc[4:6]


def backward(meta, tiles, same, other):
    return pl.pallas_call(
        backward_kernel,
        out_shape=(
            jax.ShapeDtypeStruct((2, TILE, FEAT), F32),
            jax.ShapeDtypeStruct((3, TILE, FEAT), BF16),
            jax.ShapeDtypeStruct((2, TILE, FEAT), F32),
        ),
        in_specs=[SMEM_SPEC, VMEM_SPEC] + [ANY_SPEC] * 2,
        out_specs=(VMEM_SPEC,) * 3,
        scratch_shapes=[
            pltpu.VMEM((BANDS, TILE, FEAT), BF16),
            pltpu.VMEM((WINDOW, TILE, FEAT), F32),
            pltpu.SemaphoreType.DMA((2,)),
        ],
        compiler_params=params(),
        name="backward_tiles",
    )(meta, tiles, same, other)


def relay_kernel(parity, skip, odd, out):
    p = parity[0]
    q = 1 - p
    out[p] = (skip[p] + odd[2].astype(F32)).astype(BF16)
    out[q] = skip[q].astype(BF16)


def relay_sum(parity, skip, odd):
    return pl.pallas_call(
        relay_kernel,
        out_shape=jax.ShapeDtypeStruct((2, TILE, FEAT), BF16),
        in_specs=[SMEM_SPEC] + [VMEM_SPEC] * 2,
        out_specs=VMEM_SPEC,
        compiler_params=params(),
        name="relay_sum",
    )(parity, skip, odd)


def pair_kernel(parity, own, odd, skip, mine, sibling):
    p = parity[0]
    mine[...] = own[p] + odd[p].astype(F32) + skip[p].astype(F32)
    q = 1 - p
    sibling[...] = (own[q] + odd[q].astype(F32) + skip[q].astype(F32)).astype(BF16)


def pair_sum(parity, own, odd, skip):
    return pl.pallas_call(
        pair_kernel,
        out_shape=(
            jax.ShapeDtypeStruct((TILE, FEAT), F32),
            jax.ShapeDtypeStruct((TILE, FEAT), BF16),
        ),
        in_specs=[SMEM_SPEC] + [VMEM_SPEC] * 3,
        out_specs=(VMEM_SPEC,) * 2,
        compiler_params=params(),
        name="pair_sum",
    )(parity, own, odd, skip)


def summed(parts):
    total = parts[0].astype(F32)
    for i in range(1, parts.shape[0]):
        total = total + parts[i].astype(F32)
    return total


def middle_kernel(parts, out):
    total = summed(parts)
    bias = bias_rows(total[0:4, HALF:] + total[4:8, HALF:])
    row = jnp.concatenate([total[:, :HALF].astype(BF16), bias], axis=1)
    out[...] = jnp.broadcast_to(row[None], out.shape)


def middle_sum(parts, copies):
    return pl.pallas_call(
        middle_kernel,
        out_shape=jax.ShapeDtypeStruct((copies, 16, HALF + EXTRA), BF16),
        in_specs=[VMEM_SPEC],
        out_specs=VMEM_SPEC,
        compiler_params=params(),
        name="group_sum",
    )(parts)


def last_kernel(parts, out, bias_out):
    total = summed(parts)
    out[...] = jnp.broadcast_to(total[None, :, :HALF].astype(BF16), out.shape)
    bias = total[0:4, HALF:] + total[4:8, HALF:]
    for i in range(4):
        bias_out[:, i * 128 : (i + 1) * 128] = bias[i : i + 1]


def last_sum(parts, copies):
    return pl.pallas_call(
        last_kernel,
        out_shape=(
            jax.ShapeDtypeStruct((copies, 16, HALF), BF16),
            jax.ShapeDtypeStruct((1, FEAT), F32),
        ),
        in_specs=[VMEM_SPEC],
        out_specs=(VMEM_SPEC,) * 2,
        compiler_params=params(),
        name="total_sum",
    )(parts)


def join_kernel(core, mine, other, out):
    for k in range(2):

        @pl.when(core[0] == k)
        def _():
            out[:, k * HALF : (k + 1) * HALF] = mine[...].astype(F32)
            out[:, (1 - k) * HALF : (2 - k) * HALF] = other[...].astype(F32)


def join(core, mine, other):
    return pl.pallas_call(
        join_kernel,
        out_shape=jax.ShapeDtypeStruct((FEAT, FEAT), F32),
        in_specs=[SMEM_SPEC] + [VMEM_SPEC] * 2,
        out_specs=VMEM_SPEC,
        compiler_params=params(),
        name="join_halves",
    )(core, mine, other)


def after(value, other):
    return lax.optimization_barrier((value, other))[0]


def body(features, weight, bias_vec, tile_vals, tile_coords, tile_count, cotangent):
    own_row = lax.axis_index(ROW)
    core = lax.axis_index("core")
    parity = own_row & 1
    pair_row = own_row - parity
    tiles, bias = stage(tile_vals[0, 0], bias_vec.reshape(1, FEAT))
    coords = tile_coords[0, 0]
    block = coords[:, 0]
    block_at = (block & 1 ^ core) * (BANDS // 2) + (block >> 1)
    rel = coords[:, 1] - pair_row
    below = 2 + 2 * parity
    above = 4 - 2 * parity
    panel_at = jnp.where(
        (rel >= 0) & (rel < 2),
        rel,
        jnp.where(
            (rel >= -2) & (rel < 0),
            below + rel + 2,
            jnp.where((rel >= 2) & (rel < 4), above + rel - 2, 6),
        ),
    )
    meta = jnp.concatenate([block_at, panel_at, tile_count.reshape(1)])

    own = lax.all_gather(features, PAIR, axis=0, tiled=False)
    side_row = parity.reshape(1)
    skip = moved(own, to_skip)
    odd = moved(own, to_odd)
    far = moved(pick(side_row, skip), to_odd)
    mine, theirs = forward(meta, tiles, own, odd, skip, far)
    half = (mine + swapped(theirs).astype(F32)).astype(BF16)
    parts = exchange(half, "x")
    groups = lax.axis_size(SPREAD)
    copies = lax.axis_size(REST)
    side = core.reshape(1)
    layer_out, mids, w_mine, w_theirs = dense(
        side, parts, weight, bias, cotangent, groups
    )

    same = exchange(mids, "x")
    arrived = exchange(chip_sum(w_mine, swapped(w_theirs)), SPREAD)
    other = swapped(same)
    own_g, odd_g, skip_g = backward(meta, tiles, same, other)
    arrived = after(arrived, odd_g)
    odd_in = moved(odd_g, to_odd)
    skip_out = relay_sum(side_row, skip_g, odd_in)
    skip_in = moved(skip_out, from_skip)
    keep, sibling = pair_sum(side_row, own_g, odd_in, skip_in)
    grad_features = (keep + moved(sibling, to_sibling).astype(F32)).astype(BF16)

    spread = middle_sum(arrived, copies)
    summed_in = after(exchange(spread, REST), odd_in)
    final, bias_total = last_sum(summed_in, groups)
    w_half = exchange(final, SPREAD).reshape(FEAT, HALF)
    grad_weight = join(side, w_half, swapped(w_half))
    return (layer_out, grad_weight, bias_total.reshape(FEAT), grad_features)


def solution(mesh):
    split = Mesh(mesh.devices.reshape(8, 4, 2, 4, 2), ALL)
    return jax.shard_map(
        body,
        mesh=split,
        in_specs=(
            P(ALL, None),
            P(),
            P(),
            P(ROW, COL, None, None, None),
            P(ROW, COL, None, None),
            P(ROW, COL),
            P(ALL, None),
        ),
        out_specs=(P(ALL, None), P(), P(), P(ALL, None)),
        check_vma=False,
    )
```

```python
import jax
import jax.numpy as jnp
from jax import lax
from jax.experimental import pallas as pl
from jax.experimental.pallas import tpu as pltpu
from jax.sharding import Mesh, PartitionSpec as P

REACH = 3
WINDOW = 2 * REACH + 1
TILE = 128
FEAT = 512
BANDS = 8
SLOTS = 16
ROW = ("y", "z", "pair")
COL = ("x", "core")
ALL = ROW + COL
PAIR = "pair"
SPREAD = ("z", "pair", "x")
REST = ("y",)
EXTRA = 128
HALF = 256
BF16 = jnp.bfloat16
F32 = jnp.float32
SQRT_2_OVER_PI = 0.7978845608028654
VMEM_LIMIT = 40 * 1024 * 1024

SMEM_SPEC = pl.BlockSpec(memory_space=pltpu.SMEM)
VMEM_SPEC = pl.BlockSpec(memory_space=pltpu.VMEM)
ANY_SPEC = pl.BlockSpec(memory_space=pl.ANY)
HBM_SPEC = pl.BlockSpec(memory_space=pltpu.HBM)


def params():
    return pltpu.CompilerParams(vmem_limit_bytes=VMEM_LIMIT)


def moved(block, target):
    size = lax.axis_size(ROW)
    return lax.ppermute(block, ROW, [(i, target(i) % size) for i in range(size)])


def to_sibling(i):
    return i ^ 1


def to_odd(i):
    return i + 1 if i % 2 else i - 1


def to_skip(i):
    return i + 2 if i % 2 else i - 2


def from_skip(i):
    return i - 2 if i % 2 else i + 2


def to_far(i):
    return i + 3 if i % 2 else i - 3


def swapped(block):
    return lax.ppermute(block, "core", [(0, 1), (1, 0)])


def exchange(chunks, axis):
    return lax.all_to_all(chunks, axis, 0, 0, tiled=True)


def copy_in(sources, targets, sems):
    copies = [
        pltpu.make_async_copy(s, t, sems.at[i]) for i, (s, t) in enumerate(zip(sources, targets))
    ]
    for c in copies:
        c.start()
    return copies


def stage_kernel(tiles, bias, tiles_out, bias_out, sems):
    for c in copy_in([tiles, bias], [tiles_out, bias_out], sems):
        c.wait()


def stage(tiles, bias):
    return pl.pallas_call(
        stage_kernel,
        out_shape=(
            jax.ShapeDtypeStruct(tiles.shape, tiles.dtype),
            jax.ShapeDtypeStruct(bias.shape, bias.dtype),
        ),
        in_specs=[HBM_SPEC] * 2,
        out_specs=(VMEM_SPEC,) * 2,
        scratch_shapes=[pltpu.SemaphoreType.DMA((2,))],
        compiler_params=params(),
        name="stage_tiles",
    )(tiles, bias)


def for_live_slots(count, product, add):
    def four(g, carry):
        slots = [4 * g + i for i in range(4)]
        values = [product(s) for s in slots]
        for s, v in zip(slots, values):
            add(s, v)
        return carry

    def one(s, carry):
        add(s, product(s))
        return carry

    lax.fori_loop(0, count >> 2, four, 0)
    lax.fori_loop(count & ~3, count, one, 0)


def pick_kernel(parity, skip, out):
    out[0] = skip[parity[0]]


def pick(parity, skip):
    return pl.pallas_call(
        pick_kernel,
        out_shape=jax.ShapeDtypeStruct((1, TILE, FEAT), BF16),
        in_specs=[SMEM_SPEC, VMEM_SPEC],
        out_specs=VMEM_SPEC,
        compiler_params=params(),
        name="pick_panel",
    )(parity, skip)


def forward_kernel(meta, tiles, own, odd, skip, far, mine, theirs, panels, acc, sems):
    copies = copy_in(
        [own, odd, skip, far],
        [panels.at[0:2], panels.at[2:4], panels.at[4:6], panels.at[6:7]],
        sems,
    )
    acc[...] = jnp.zeros_like(acc)
    for c in copies:
        c.wait()

    def product(s):
        return jnp.dot(tiles[s], panels[meta[SLOTS + s]], preferred_element_type=F32)

    def add(s, value):
        acc[meta[s]] += value

    for_live_slots(meta[2 * SLOTS], product, add)
    mine[...] = acc[0:4]
    theirs[...] = acc[4:8].astype(BF16)


def forward(meta, tiles, own, odd, skip, far):
    return pl.pallas_call(
        forward_kernel,
        out_shape=(
            jax.ShapeDtypeStruct((BANDS // 2, TILE, FEAT), F32),
            jax.ShapeDtypeStruct((BANDS // 2, TILE, FEAT), BF16),
        ),
        in_specs=[SMEM_SPEC, VMEM_SPEC] + [ANY_SPEC] * 4,
        out_specs=(VMEM_SPEC,) * 2,
        scratch_shapes=[
            pltpu.VMEM((WINDOW, TILE, FEAT), BF16),
            pltpu.VMEM((BANDS, TILE, FEAT), F32),
            pltpu.SemaphoreType.DMA((4,)),
        ],
        compiler_params=params(),
        name="aggregate_tiles",
    )(meta, tiles, own, odd, skip, far)


def bias_rows(total):
    high = total.astype(BF16).astype(F32)
    return jnp.concatenate([high, total - high, jnp.zeros((8, 128), F32)], axis=0).astype(BF16)


def dense_kernel(parts, weight, bias, cot, layer_out, mids, agg_out, pre_out):
    agg = parts[0].astype(F32)
    for i in range(1, BANDS // 2):
        agg = agg + parts[i].astype(F32)
    agg_b = agg.astype(BF16)
    agg_out[...] = agg_b
    w = weight[...]
    v = jnp.dot(agg_b, w, preferred_element_type=F32) + bias[...]
    v2 = v * v
    t = jnp.tanh(SQRT_2_OVER_PI * (v + 0.044715 * (v2 * v)))
    half = 0.5 * (1.0 + t)
    layer_out[...] = (v * half).astype(BF16)
    slope = half + 0.5 * v * (1.0 - t * t) * (SQRT_2_OVER_PI * (1.0 + 3 * 0.044715 * v2))
    grad_pre = (cot[...].astype(F32) * slope).astype(BF16)
    pre_out[...] = grad_pre
    mid = lax.dot_general(
        grad_pre, w, (((1,), (1,)), ((), ())), preferred_element_type=F32
    ).astype(BF16)
    mids[...] = jnp.broadcast_to(mid[None], mids.shape)


def dense(parts, weight, bias, cot):
    return pl.pallas_call(
        dense_kernel,
        out_shape=(
            jax.ShapeDtypeStruct((TILE, FEAT), BF16),
            jax.ShapeDtypeStruct((BANDS // 2, TILE, FEAT), BF16),
            jax.ShapeDtypeStruct((TILE, FEAT), BF16),
            jax.ShapeDtypeStruct((TILE, FEAT), BF16),
        ),
        in_specs=[VMEM_SPEC] * 4,
        out_specs=(VMEM_SPEC,) * 4,
        compiler_params=params(),
        name="dense_layer",
    )(parts, weight, bias, cot)


def term_kernel(core, agg_b, grad_pre, mine, theirs, terms):
    term = lax.dot_general(
        agg_b[...], grad_pre[...], (((0,), (0,)), ((), ())), preferred_element_type=F32
    )
    count = mine.shape[0] - 1
    for i in range(2):
        terms[i] = term[:, i * HALF : (i + 1) * HALF].reshape(count, 16, HALF)
    k = core[0]
    mine[0:count] = terms[k]
    theirs[0:count] = terms[1 - k].astype(BF16)
    total = jnp.sum(grad_pre[...].astype(F32), axis=0, keepdims=True)
    total = jnp.concatenate([total[:, i * 128 : (i + 1) * 128] for i in range(4)], axis=0)
    zeros = jnp.zeros((16, HALF - EXTRA), F32)
    mine[count] = jnp.concatenate([bias_rows(total).astype(F32), zeros], axis=1)
    theirs[count] = jnp.concatenate([bias_rows(total), zeros.astype(BF16)], axis=1)


def weight_term(core, agg_b, grad_pre, groups):
    return pl.pallas_call(
        term_kernel,
        out_shape=(
            jax.ShapeDtypeStruct((groups + 1, 16, HALF), F32),
            jax.ShapeDtypeStruct((groups + 1, 16, HALF), BF16),
        ),
        in_specs=[SMEM_SPEC] + [VMEM_SPEC] * 2,
        out_specs=(VMEM_SPEC,) * 2,
        scratch_shapes=[pltpu.VMEM((2, groups, 16, HALF), F32)],
        compiler_params=params(),
        name="weight_term",
    )(core, agg_b, grad_pre)


def chip_kernel(mine, theirs, out):
    count = out.shape[0]
    out[:, :, :HALF] = (mine[0:count] + theirs[0:count].astype(F32)).astype(BF16)
    both = mine[count, :, :EXTRA] + theirs[count, :, :EXTRA].astype(F32)
    bias = bias_rows(both[0:4] + both[4:8])
    out[:, :, HALF:] = jnp.broadcast_to(bias[None], (count, 16, EXTRA))


def chip_sum(mine, theirs):
    count = mine.shape[0] - 1
    return pl.pallas_call(
        chip_kernel,
        out_shape=jax.ShapeDtypeStruct((count, 16, HALF + EXTRA), BF16),
        in_specs=[VMEM_SPEC] * 2,
        out_specs=VMEM_SPEC,
        compiler_params=params(),
        name="chip_sum",
    )(mine, theirs)


def backward_kernel(meta, tiles, same, other, own, odd, skip, acc):
    acc[...] = jnp.zeros_like(acc)

    def product(s):
        b = meta[s]
        panel = lax.select(b < BANDS // 2, same[b & 3], other[b & 3])
        return lax.dot_general(
            tiles[s], panel, (((0,), (0,)), ((), ())), preferred_element_type=F32
        )

    def add(s, value):
        acc[meta[SLOTS + s]] += value

    for_live_slots(meta[2 * SLOTS], product, add)
    own[...] = acc[0:2]
    odd[0:2] = acc[2:4].astype(BF16)
    odd[2:3] = acc[6:7].astype(BF16)
    skip[...] = acc[4:6]


def backward(meta, tiles, same, other):
    return pl.pallas_call(
        backward_kernel,
        out_shape=(
            jax.ShapeDtypeStruct((2, TILE, FEAT), F32),
            jax.ShapeDtypeStruct((3, TILE, FEAT), BF16),
            jax.ShapeDtypeStruct((2, TILE, FEAT), F32),
        ),
        in_specs=[SMEM_SPEC] + [VMEM_SPEC] * 3,
        out_specs=(VMEM_SPEC,) * 3,
        scratch_shapes=[
            pltpu.VMEM((WINDOW, TILE, FEAT), F32),
        ],
        compiler_params=params(),
        name="backward_tiles",
    )(meta, tiles, same, other)


def relay_kernel(parity, skip, odd, out):
    p = parity[0]
    q = 1 - p
    out[p] = (skip[p] + odd[2].astype(F32)).astype(BF16)
    out[q] = skip[q].astype(BF16)


def relay_sum(parity, skip, odd):
    return pl.pallas_call(
        relay_kernel,
        out_shape=jax.ShapeDtypeStruct((2, TILE, FEAT), BF16),
        in_specs=[SMEM_SPEC] + [VMEM_SPEC] * 2,
        out_specs=VMEM_SPEC,
        compiler_params=params(),
        name="relay_sum",
    )(parity, skip, odd)


def pair_kernel(parity, own, odd, skip, mine, sibling):
    p = parity[0]
    mine[...] = own[p] + odd[p].astype(F32) + skip[p].astype(F32)
    q = 1 - p
    sibling[...] = (own[q] + odd[q].astype(F32) + skip[q].astype(F32)).astype(BF16)


def pair_sum(parity, own, odd, skip):
    return pl.pallas_call(
        pair_kernel,
        out_shape=(
            jax.ShapeDtypeStruct((TILE, FEAT), F32),
            jax.ShapeDtypeStruct((TILE, FEAT), BF16),
        ),
        in_specs=[SMEM_SPEC] + [VMEM_SPEC] * 3,
        out_specs=(VMEM_SPEC,) * 2,
        compiler_params=params(),
        name="pair_sum",
    )(parity, own, odd, skip)


def summed(parts):
    total = parts[0].astype(F32)
    for i in range(1, parts.shape[0]):
        total = total + parts[i].astype(F32)
    return total


def middle_kernel(parts, out):
    total = summed(parts)
    bias = bias_rows(total[0:4, HALF:] + total[4:8, HALF:])
    row = jnp.concatenate([total[:, :HALF].astype(BF16), bias], axis=1)
    out[...] = jnp.broadcast_to(row[None], out.shape)


def middle_sum(parts, copies):
    return pl.pallas_call(
        middle_kernel,
        out_shape=jax.ShapeDtypeStruct((copies, 16, HALF + EXTRA), BF16),
        in_specs=[VMEM_SPEC],
        out_specs=VMEM_SPEC,
        compiler_params=params(),
        name="group_sum",
    )(parts)


def last_kernel(parts, out, bias_out):
    total = summed(parts)
    out[...] = jnp.broadcast_to(total[None, :, :HALF].astype(BF16), out.shape)
    bias = total[0:4, HALF:] + total[4:8, HALF:]
    for i in range(4):
        bias_out[:, i * 128 : (i + 1) * 128] = bias[i : i + 1]


def last_sum(parts, copies):
    return pl.pallas_call(
        last_kernel,
        out_shape=(
            jax.ShapeDtypeStruct((copies, 16, HALF), BF16),
            jax.ShapeDtypeStruct((1, FEAT), F32),
        ),
        in_specs=[VMEM_SPEC],
        out_specs=(VMEM_SPEC,) * 2,
        compiler_params=params(),
        name="total_sum",
    )(parts)


def join_kernel(core, mine, other, out):
    for k in range(2):

        @pl.when(core[0] == k)
        def _():
            out[:, k * HALF : (k + 1) * HALF] = mine[...].astype(F32)
            out[:, (1 - k) * HALF : (2 - k) * HALF] = other[...].astype(F32)


def join(core, mine, other):
    return pl.pallas_call(
        join_kernel,
        out_shape=jax.ShapeDtypeStruct((FEAT, FEAT), F32),
        in_specs=[SMEM_SPEC] + [VMEM_SPEC] * 2,
        out_specs=VMEM_SPEC,
        compiler_params=params(),
        name="join_halves",
    )(core, mine, other)


def after(value, other):
    return lax.optimization_barrier((value, other))[0]


def body(features, weight, bias_vec, tile_vals, tile_coords, tile_count, cotangent):
    own_row = lax.axis_index(ROW)
    core = lax.axis_index("core")
    parity = own_row & 1
    pair_row = own_row - parity
    tiles, bias = stage(tile_vals[0, 0], bias_vec.reshape(1, FEAT))
    coords = tile_coords[0, 0]
    block = coords[:, 0]
    block_at = (block & 1 ^ core) * (BANDS // 2) + (block >> 1)
    rel = coords[:, 1] - pair_row
    below = 2 + 2 * parity
    above = 4 - 2 * parity
    panel_at = jnp.where(
        (rel >= 0) & (rel < 2),
        rel,
        jnp.where(
            (rel >= -2) & (rel < 0),
            below + rel + 2,
            jnp.where((rel >= 2) & (rel < 4), above + rel - 2, 6),
        ),
    )
    meta = jnp.concatenate([block_at, panel_at, tile_count.reshape(1)])

    own = lax.all_gather(features, PAIR, axis=0, tiled=False)
    side_row = parity.reshape(1)
    skip = moved(own, to_skip)
    odd = moved(own, to_odd)
    far = moved(pick(side_row, skip), to_odd)
    mine, theirs = forward(meta, tiles, own, odd, skip, far)
    half = (mine + swapped(theirs).astype(F32)).astype(BF16)
    parts = exchange(half, "x")
    groups = lax.axis_size(SPREAD)
    copies = lax.axis_size(REST)
    side = core.reshape(1)
    layer_out, mids, agg_b, grad_pre = dense(parts, weight, bias, cotangent)
    w_mine, w_theirs = weight_term(side, agg_b, grad_pre, groups)

    same = exchange(mids, "x")
    arrived = exchange(chip_sum(w_mine, swapped(w_theirs)), SPREAD)
    other = swapped(same)
    own_g, odd_g, skip_g = backward(meta, tiles, same, other)
    arrived = after(arrived, odd_g)
    odd_in = moved(odd_g, to_odd)
    skip_out = relay_sum(side_row, skip_g, odd_in)
    skip_in = moved(skip_out, from_skip)
    keep, sibling = pair_sum(side_row, own_g, odd_in, skip_in)
    grad_features = (keep + moved(sibling, to_sibling).astype(F32)).astype(BF16)

    spread = middle_sum(arrived, copies)
    summed_in = after(exchange(spread, REST), odd_in)
    final, bias_total = last_sum(summed_in, groups)
    w_half = exchange(final, SPREAD).reshape(FEAT, HALF)
    grad_weight = join(side, w_half, swapped(w_half))
    return (layer_out, grad_weight, bias_total.reshape(FEAT), grad_features)


def solution(mesh):
    split = Mesh(mesh.devices.reshape(8, 4, 2, 4, 2), ALL)
    return jax.shard_map(
        body,
        mesh=split,
        in_specs=(
            P(ALL, None),
            P(),
            P(),
            P(ROW, COL, None, None, None),
            P(ROW, COL, None, None),
            P(ROW, COL),
            P(ALL, None),
        ),
        out_specs=(P(ALL, None), P(), P(), P(ALL, None)),
        check_vma=False,
    )
```

```python
import jax
import jax.numpy as jnp
from jax import lax
from jax.experimental import pallas as pl
from jax.experimental.pallas import tpu as pltpu
from jax.sharding import Mesh, PartitionSpec as P

REACH = 3
WINDOW = 2 * REACH + 1
TILE = 128
FEAT = 512
BANDS = 8
SLOTS = 16
ROW = ("y", "z", "pair")
COL = ("x", "core")
ALL = ROW + COL
PAIR = "pair"
SPREAD = ("z", "pair", "x")
REST = ("y",)
EXTRA = 128
HALF = 256
BF16 = jnp.bfloat16
F32 = jnp.float32
SQRT_2_OVER_PI = 0.7978845608028654
VMEM_LIMIT = 40 * 1024 * 1024

SMEM_SPEC = pl.BlockSpec(memory_space=pltpu.SMEM)
VMEM_SPEC = pl.BlockSpec(memory_space=pltpu.VMEM)
ANY_SPEC = pl.BlockSpec(memory_space=pl.ANY)
HBM_SPEC = pl.BlockSpec(memory_space=pltpu.HBM)


def params():
    return pltpu.CompilerParams(vmem_limit_bytes=VMEM_LIMIT)


def moved(block, target):
    size = lax.axis_size(ROW)
    return lax.ppermute(block, ROW, [(i, target(i) % size) for i in range(size)])


def to_sibling(i):
    return i ^ 1


def to_odd(i):
    return i + 1 if i % 2 else i - 1


def to_skip(i):
    return i + 2 if i % 2 else i - 2


def from_skip(i):
    return i - 2 if i % 2 else i + 2


def to_far(i):
    return i + 3 if i % 2 else i - 3


def swapped(block):
    return lax.ppermute(block, "core", [(0, 1), (1, 0)])


def exchange(chunks, axis):
    return lax.all_to_all(chunks, axis, 0, 0, tiled=True)


def copy_in(sources, targets, sems):
    copies = [
        pltpu.make_async_copy(s, t, sems.at[i]) for i, (s, t) in enumerate(zip(sources, targets))
    ]
    for c in copies:
        c.start()
    return copies


def stage_kernel(tiles, bias, tiles_out, bias_out, sems):
    for c in copy_in([tiles, bias], [tiles_out, bias_out], sems):
        c.wait()


def stage(tiles, bias):
    return pl.pallas_call(
        stage_kernel,
        out_shape=(
            jax.ShapeDtypeStruct(tiles.shape, tiles.dtype),
            jax.ShapeDtypeStruct(bias.shape, bias.dtype),
        ),
        in_specs=[HBM_SPEC] * 2,
        out_specs=(VMEM_SPEC,) * 2,
        scratch_shapes=[pltpu.SemaphoreType.DMA((2,))],
        compiler_params=params(),
        name="stage_tiles",
    )(tiles, bias)


def for_live_slots(count, product, add):
    def four(g, carry):
        slots = [4 * g + i for i in range(4)]
        values = [product(s) for s in slots]
        for s, v in zip(slots, values):
            add(s, v)
        return carry

    def one(s, carry):
        add(s, product(s))
        return carry

    lax.fori_loop(0, count >> 2, four, 0)
    lax.fori_loop(count & ~3, count, one, 0)


def pick_kernel(parity, skip, out):
    out[0] = skip[parity[0]]


def pick(parity, skip):
    return pl.pallas_call(
        pick_kernel,
        out_shape=jax.ShapeDtypeStruct((1, TILE, FEAT), BF16),
        in_specs=[SMEM_SPEC, VMEM_SPEC],
        out_specs=VMEM_SPEC,
        compiler_params=params(),
        name="pick_panel",
    )(parity, skip)


def forward_kernel(meta, tiles, own, odd, skip, far, mine, theirs, panels, acc, sems):
    copies = copy_in(
        [own, odd, skip, far],
        [panels.at[0:2], panels.at[2:4], panels.at[4:6], panels.at[6:7]],
        sems,
    )
    acc[...] = jnp.zeros_like(acc)
    for c in copies:
        c.wait()

    def product(s):
        return jnp.dot(tiles[s], panels[meta[SLOTS + s]], preferred_element_type=F32)

    def add(s, value):
        acc[meta[s]] += value

    for_live_slots(meta[2 * SLOTS], product, add)
    mine[...] = acc[0:4]
    theirs[...] = acc[4:8].astype(BF16)


def forward(meta, tiles, own, odd, skip, far):
    return pl.pallas_call(
        forward_kernel,
        out_shape=(
            jax.ShapeDtypeStruct((BANDS // 2, TILE, FEAT), F32),
            jax.ShapeDtypeStruct((BANDS // 2, TILE, FEAT), BF16),
        ),
        in_specs=[SMEM_SPEC, VMEM_SPEC] + [ANY_SPEC] * 4,
        out_specs=(VMEM_SPEC,) * 2,
        scratch_shapes=[
            pltpu.VMEM((WINDOW, TILE, FEAT), BF16),
            pltpu.VMEM((BANDS, TILE, FEAT), F32),
            pltpu.SemaphoreType.DMA((4,)),
        ],
        compiler_params=params(),
        name="aggregate_tiles",
    )(meta, tiles, own, odd, skip, far)


def bias_rows(total):
    high = total.astype(BF16).astype(F32)
    return jnp.concatenate([high, total - high, jnp.zeros((8, 128), F32)], axis=0).astype(BF16)


def dense_kernel(core, parts, weight, bias, cot, layer_out, mids, mine, theirs, terms):
    agg = parts[0].astype(F32)
    for i in range(1, BANDS // 2):
        agg = agg + parts[i].astype(F32)
    agg_b = agg.astype(BF16)
    w = weight[...]
    v = jnp.dot(agg_b, w, preferred_element_type=F32) + bias[...]
    v2 = v * v
    t = jnp.tanh(SQRT_2_OVER_PI * (v + 0.044715 * (v2 * v)))
    half = 0.5 * (1.0 + t)
    layer_out[...] = (v * half).astype(BF16)
    slope = half + 0.5 * v * (1.0 - t * t) * (SQRT_2_OVER_PI * (1.0 + 3 * 0.044715 * v2))
    grad_pre = (cot[...].astype(F32) * slope).astype(BF16)
    mid = lax.dot_general(
        grad_pre, w, (((1,), (1,)), ((), ())), preferred_element_type=F32
    ).astype(BF16)
    mids[...] = jnp.broadcast_to(mid[None], mids.shape)
    term = lax.dot_general(agg_b, grad_pre, (((0,), (0,)), ((), ())), preferred_element_type=F32)
    count = mine.shape[0] - 1
    for i in range(2):
        terms[i] = term[:, i * HALF : (i + 1) * HALF].reshape(count, 16, HALF)
    k = core[0]
    mine[0:count] = terms[k]
    theirs[0:count] = terms[1 - k].astype(BF16)
    total = jnp.sum(grad_pre.astype(F32), axis=0, keepdims=True)
    total = jnp.concatenate([total[:, i * 128 : (i + 1) * 128] for i in range(4)], axis=0)
    zeros = jnp.zeros((16, HALF - EXTRA), F32)
    mine[count] = jnp.concatenate([bias_rows(total).astype(F32), zeros], axis=1)
    theirs[count] = jnp.concatenate([bias_rows(total), zeros.astype(BF16)], axis=1)


def dense(core, parts, weight, bias, cot, groups):
    return pl.pallas_call(
        dense_kernel,
        out_shape=(
            jax.ShapeDtypeStruct((TILE, FEAT), BF16),
            jax.ShapeDtypeStruct((BANDS // 2, TILE, FEAT), BF16),
            jax.ShapeDtypeStruct((groups + 1, 16, HALF), F32),
            jax.ShapeDtypeStruct((groups + 1, 16, HALF), BF16),
        ),
        in_specs=[SMEM_SPEC] + [VMEM_SPEC] * 4,
        out_specs=(VMEM_SPEC,) * 4,
        scratch_shapes=[pltpu.VMEM((2, groups, 16, HALF), F32)],
        compiler_params=params(),
        name="dense_layer",
    )(core, parts, weight, bias, cot)


def chip_kernel(mine, theirs, out):
    count = out.shape[0]
    out[:, :, :HALF] = (mine[0:count] + theirs[0:count].astype(F32)).astype(BF16)
    both = mine[count, :, :EXTRA] + theirs[count, :, :EXTRA].astype(F32)
    bias = bias_rows(both[0:4] + both[4:8])
    out[:, :, HALF:] = jnp.broadcast_to(bias[None], (count, 16, EXTRA))


def chip_sum(mine, theirs):
    count = mine.shape[0] - 1
    return pl.pallas_call(
        chip_kernel,
        out_shape=jax.ShapeDtypeStruct((count, 16, HALF + EXTRA), BF16),
        in_specs=[VMEM_SPEC] * 2,
        out_specs=VMEM_SPEC,
        compiler_params=params(),
        name="chip_sum",
    )(mine, theirs)


def backward_kernel(meta, tiles, same, other, own, odd, skip, acc):
    acc[...] = jnp.zeros_like(acc)

    def product(s):
        b = meta[s]
        panel = lax.select(b < BANDS // 2, same[b & 3], other[b & 3])
        return lax.dot_general(
            tiles[s], panel, (((0,), (0,)), ((), ())), preferred_element_type=F32
        )

    def add(s, value):
        acc[meta[SLOTS + s]] += value

    for_live_slots(meta[2 * SLOTS], product, add)
    own[...] = acc[0:2]
    odd[0:2] = acc[2:4].astype(BF16)
    odd[2:3] = acc[6:7].astype(BF16)
    skip[...] = acc[4:6]


def backward(meta, tiles, same, other):
    return pl.pallas_call(
        backward_kernel,
        out_shape=(
            jax.ShapeDtypeStruct((2, TILE, FEAT), F32),
            jax.ShapeDtypeStruct((3, TILE, FEAT), BF16),
            jax.ShapeDtypeStruct((2, TILE, FEAT), F32),
        ),
        in_specs=[SMEM_SPEC] + [VMEM_SPEC] * 3,
        out_specs=(VMEM_SPEC,) * 3,
        scratch_shapes=[
            pltpu.VMEM((WINDOW, TILE, FEAT), F32),
        ],
        compiler_params=params(),
        name="backward_tiles",
    )(meta, tiles, same, other)


def relay_kernel(parity, skip, odd, out):
    p = parity[0]
    q = 1 - p
    out[p] = (skip[p] + odd[2].astype(F32)).astype(BF16)
    out[q] = skip[q].astype(BF16)


def relay_sum(parity, skip, odd):
    return pl.pallas_call(
        relay_kernel,
        out_shape=jax.ShapeDtypeStruct((2, TILE, FEAT), BF16),
        in_specs=[SMEM_SPEC] + [VMEM_SPEC] * 2,
        out_specs=VMEM_SPEC,
        compiler_params=params(),
        name="relay_sum",
    )(parity, skip, odd)


def pair_kernel(parity, own, odd, skip, mine, sibling):
    p = parity[0]
    mine[...] = own[p] + odd[p].astype(F32) + skip[p].astype(F32)
    q = 1 - p
    sibling[...] = (own[q] + odd[q].astype(F32) + skip[q].astype(F32)).astype(BF16)


def pair_sum(parity, own, odd, skip):
    return pl.pallas_call(
        pair_kernel,
        out_shape=(
            jax.ShapeDtypeStruct((TILE, FEAT), F32),
            jax.ShapeDtypeStruct((TILE, FEAT), BF16),
        ),
        in_specs=[SMEM_SPEC] + [VMEM_SPEC] * 3,
        out_specs=(VMEM_SPEC,) * 2,
        compiler_params=params(),
        name="pair_sum",
    )(parity, own, odd, skip)


def summed(parts):
    total = parts[0].astype(F32)
    for i in range(1, parts.shape[0]):
        total = total + parts[i].astype(F32)
    return total


def middle_kernel(parts, out):
    total = summed(parts)
    bias = bias_rows(total[0:4, HALF:] + total[4:8, HALF:])
    row = jnp.concatenate([total[:, :HALF].astype(BF16), bias], axis=1)
    out[...] = jnp.broadcast_to(row[None], out.shape)


def middle_sum(parts, copies):
    return pl.pallas_call(
        middle_kernel,
        out_shape=jax.ShapeDtypeStruct((copies, 16, HALF + EXTRA), BF16),
        in_specs=[VMEM_SPEC],
        out_specs=VMEM_SPEC,
        compiler_params=params(),
        name="group_sum",
    )(parts)


def last_kernel(parts, out, bias_out):
    total = summed(parts)
    out[...] = jnp.broadcast_to(total[None, :, :HALF].astype(BF16), out.shape)
    bias = total[0:4, HALF:] + total[4:8, HALF:]
    for i in range(4):
        bias_out[:, i * 128 : (i + 1) * 128] = bias[i : i + 1]


def last_sum(parts, copies):
    return pl.pallas_call(
        last_kernel,
        out_shape=(
            jax.ShapeDtypeStruct((copies, 16, HALF), BF16),
            jax.ShapeDtypeStruct((1, FEAT), F32),
        ),
        in_specs=[VMEM_SPEC],
        out_specs=(VMEM_SPEC,) * 2,
        compiler_params=params(),
        name="total_sum",
    )(parts)


def join_kernel(core, mine, other, out):
    for k in range(2):

        @pl.when(core[0] == k)
        def _():
            out[:, k * HALF : (k + 1) * HALF] = mine[...].astype(F32)
            out[:, (1 - k) * HALF : (2 - k) * HALF] = other[...].astype(F32)


def join(core, mine, other):
    return pl.pallas_call(
        join_kernel,
        out_shape=jax.ShapeDtypeStruct((FEAT, FEAT), F32),
        in_specs=[SMEM_SPEC] + [VMEM_SPEC] * 2,
        out_specs=VMEM_SPEC,
        compiler_params=params(),
        name="join_halves",
    )(core, mine, other)


def after(value, other):
    return lax.optimization_barrier((value, other))[0]


def body(features, weight, bias_vec, tile_vals, tile_coords, tile_count, cotangent):
    own_row = lax.axis_index(ROW)
    core = lax.axis_index("core")
    parity = own_row & 1
    pair_row = own_row - parity
    tiles, bias = stage(tile_vals[0, 0], bias_vec.reshape(1, FEAT))
    coords = tile_coords[0, 0]
    block = coords[:, 0]
    block_at = (block & 1 ^ core) * (BANDS // 2) + (block >> 1)
    rel = coords[:, 1] - pair_row
    below = 2 + 2 * parity
    above = 4 - 2 * parity
    panel_at = jnp.where(
        (rel >= 0) & (rel < 2),
        rel,
        jnp.where(
            (rel >= -2) & (rel < 0),
            below + rel + 2,
            jnp.where((rel >= 2) & (rel < 4), above + rel - 2, 6),
        ),
    )
    meta = jnp.concatenate([block_at, panel_at, tile_count.reshape(1)])

    own = lax.all_gather(features, PAIR, axis=0, tiled=False)
    side_row = parity.reshape(1)
    skip = moved(own, to_skip)
    odd = moved(own, to_odd)
    far = moved(pick(side_row, skip), to_odd)
    mine, theirs = forward(meta, tiles, own, odd, skip, far)
    half = (mine + swapped(theirs).astype(F32)).astype(BF16)
    parts = exchange(half, "x")
    groups = lax.axis_size(SPREAD)
    copies = lax.axis_size(REST)
    side = core.reshape(1)
    layer_out, mids, w_mine, w_theirs = dense(
        side, parts, weight, bias, cotangent, groups
    )

    same = exchange(mids, "x")
    arrived = exchange(chip_sum(w_mine, swapped(w_theirs)), SPREAD)
    other = swapped(same)
    own_g, odd_g, skip_g = backward(meta, tiles, same, other)
    arrived = after(arrived, odd_g)
    odd_in = moved(odd_g, to_odd)
    skip_out = relay_sum(side_row, skip_g, odd_in)
    skip_in = moved(skip_out, from_skip)
    keep, sibling = pair_sum(side_row, own_g, odd_in, skip_in)
    grad_features = (keep + moved(sibling, to_sibling).astype(F32)).astype(BF16)

    spread = middle_sum(arrived, copies)
    summed_in = after(exchange(spread, REST), odd_in)
    final, bias_total = last_sum(summed_in, groups)
    w_half = exchange(final, SPREAD).reshape(FEAT, HALF)
    grad_weight = join(side, w_half, swapped(w_half))
    return (layer_out, grad_weight, bias_total.reshape(FEAT), grad_features)


def solution(mesh):
    split = Mesh(mesh.devices.reshape(8, 4, 2, 4, 2), ALL)
    return jax.shard_map(
        body,
        mesh=split,
        in_specs=(
            P(ALL, None),
            P(),
            P(),
            P(ROW, COL, None, None, None),
            P(ROW, COL, None, None),
            P(ROW, COL),
            P(ALL, None),
        ),
        out_specs=(P(ALL, None), P(), P(), P(ALL, None)),
        check_vma=False,
    )
```
